256 devices in a mesh: leaf: 64 (over x, z, core), cpl: 4 (over y).
Axes of the slice: x: 4, y: 4, z: 8, core: 2. Of those that a mesh axis runs over, the one named last changes fastest.
Arguments:
- vectors: bfloat16 [65536, 64], P('leaf'), may hold values from -6 to 6
- embeddings: bfloat16 [65536, 64], P('leaf'), may hold values from -2 to 2
- basis: bfloat16 [65536, 64], P('leaf'), may hold values from -0.75 to 0.75
- transfer: bfloat16 [1984, 64, 64], P('leaf'), may hold values from -0.5 to 0.5
- coupling: bfloat16 [65536, 64, 64], P(('leaf', 'cpl')), may hold values from -0.125 to 0.125
- top_transfer: bfloat16 [62, 64, 64], replicated, may hold values from -0.5 to 0.5
- top_coupling: bfloat16 [62, 64, 64], replicated, may hold values from -3 to 3
- send_boxes: int32 [64, 4, 128], P('leaf', 'cpl'), may hold values from 0 to 30, as said below
- block_slot: int32 [65536], P(('leaf', 'cpl')), may hold values from 0 to 127, as said below
- block_target: int32 [65536], P(('leaf', 'cpl')), may hold values from 0 to 31, as said below
Outputs:
- potentials: float32 [65536, 64], P(('leaf', 'cpl'))
The draws below stay inside these ranges and needn't reach their ends.
Inputs may be any that keep to these rules, and one draw needn't show every extreme that they name: send_boxes[p, q, d * 2 + k] is the box of subtree p that leaf device p sends to leaf device d in slot k for the blocks of cpl index q, numbered as in the reference program. block_slot of a block is a slot p * 2 + k received from leaf device p. Of the 2 slots from one device to another, the ones that live blocks read come first; one device reads all 128 slots. `block_target`: A live block adds to a box at the same level of its subtree as the box that its slot carries; 31 marks an empty block. On every leaf device, one cpl index holds no empty block.
All inputs are finite; a program needn't handle non-finite values.
Results may differ from the reference program's by a relative error of at most 0.0029.
Values may be sent and summed in bfloat16 or wider, within the bound.
A program may use at most 128 MiB of HBM per device.

```python
import math
import jax
import jax.numpy as jnp
from jax import lax

RANK = 64
NRHS = 64
EMB = 64
LEAF = 64
B_DEV = 16
CAP = 2
BLK_DEV = 256
NODES_DEV = 31
LEAVES = 1024
ITEMS = 65536
SLOTS = 128
BOXES = 1984
BLOCKS = 65536
TOPS = 62
TOPL = 6
SUBL = 4
N_LEAF = 64
N_CPL = 4


def shuffled(owner_key):
    return jax.random.permutation(owner_key, BLK_DEV).astype(jnp.int32)


def plan_tables(key):
    key_list = jax.random.split(key, 10)
    slot_count = N_LEAF * CAP
    box_count = 2 * B_DEV - 1
    sending = jax.random.randint(key_list[0], (N_LEAF, N_CPL, slot_count), 0, box_count, dtype=jnp.int32)
    used_pairs = jax.random.randint(key_list[1], (N_LEAF, N_CPL, N_LEAF), 1, CAP + 1, dtype=jnp.int32)
    full_device = jax.random.randint(key_list[2], (), 0, N_LEAF, dtype=jnp.int32)
    full_column = jax.random.randint(key_list[3], (), 0, N_CPL, dtype=jnp.int32)
    is_full = (jnp.arange(N_CPL, dtype=jnp.int32)[None, :, None] == full_column) & (jnp.arange(N_LEAF, dtype=jnp.int32)[None, None, :] == full_device)
    used_pairs = jnp.where(is_full, CAP, used_pairs)
    received_counts = jnp.transpose(used_pairs, (2, 1, 0))
    slot_within = jnp.arange(CAP, dtype=jnp.int32)
    live_slot = (slot_within[None, None, None, :] < received_counts[:, :, :, None]).reshape(N_LEAF, N_CPL, slot_count)
    boxes_seen = jnp.transpose(sending.reshape(N_LEAF, N_CPL, N_LEAF, CAP), (2, 1, 0, 3)).reshape(N_LEAF, N_CPL, slot_count)
    dead_flags = 1 - live_slot.astype(jnp.int32)
    order_used = jnp.argsort(dead_flags, axis=-1, stable=True).astype(jnp.int32)
    used_count = jnp.sum(live_slot.astype(jnp.int32), axis=-1)
    heavy_column = jax.random.randint(key_list[4], (N_LEAF,), 0, N_CPL, dtype=jnp.int32)
    floor_live = min(max(slot_count, 2 * BLK_DEV // 5), BLK_DEV - 1)
    live_count = jax.random.randint(key_list[5], (N_LEAF, N_CPL), floor_live, BLK_DEV, dtype=jnp.int32)
    live_count = jnp.where(jnp.arange(N_CPL, dtype=jnp.int32)[None, :] == heavy_column[:, None], BLK_DEV, live_count)
    ranks = jax.vmap(shuffled)(jax.random.split(key_list[6], N_LEAF * N_CPL)).reshape(N_LEAF, N_CPL, BLK_DEV)
    extra_pick = jax.random.randint(key_list[7], (N_LEAF, N_CPL, BLK_DEV), 0, jnp.maximum(used_count, 1)[:, :, None], dtype=jnp.int32)
    chosen = jnp.where(ranks < used_count[:, :, None], ranks, extra_pick)
    live_slot_index = jnp.take_along_axis(order_used, jnp.minimum(chosen, slot_count - 1), axis=-1)
    spare_slot = jax.random.randint(key_list[8], (N_LEAF, N_CPL, BLK_DEV), 0, slot_count, dtype=jnp.int32)
    is_live = ranks < live_count[:, :, None]
    slot_final = jnp.where(is_live, live_slot_index, spare_slot)
    source_box = jnp.take_along_axis(boxes_seen, slot_final, axis=-1)
    level_index = jnp.zeros_like(source_box)
    for exponent in range(1, B_DEV.bit_length()):
        level_index = level_index + (source_box + 1 >= 1 << exponent).astype(jnp.int32)
    level_width = jnp.left_shift(jnp.ones_like(level_index), level_index)
    placed = jax.random.randint(key_list[9], level_index.shape, 0, level_width, dtype=jnp.int32)
    target_final = jnp.where(is_live, level_width - 1 + placed, box_count)
    return (sending, slot_final.reshape(-1).astype(jnp.int32), target_final.reshape(-1).astype(jnp.int32))


def draw_send_boxes(key, part):
    tables = plan_tables(jax.random.fold_in(key, 5))
    return tables[0]


def draw_block_slot(key, part):
    tables = plan_tables(jax.random.fold_in(key, 5))
    return tables[1]


def draw_block_target(key, part):
    tables = plan_tables(jax.random.fold_in(key, 5))
    return tables[2]


def draw_embeddings(key, part):
    key = jax.random.fold_in(key, 7)
    key_scale, key_direction = jax.random.split(key)
    log_scale = jax.random.uniform(key_scale, (ITEMS, 1), jnp.float32, math.log(0.25), math.log(2.0))
    direction = jax.random.truncated_normal(key_direction, -4.0, 4.0, (ITEMS, EMB), jnp.float32)
    return (jnp.exp(log_scale) * direction / math.sqrt(EMB)).astype(jnp.bfloat16)


def level_of(key, extent, cuts, smallest, high):
    gain = 1.0
    for position, blocks in cuts:
        steps = jax.random.uniform(jax.random.fold_in(jax.random.fold_in(key, 6), position), (blocks,), jnp.float32, smallest / len(cuts), high / len(cuts))
        gain = gain * jnp.repeat(jnp.exp(steps), extent[position] // blocks).reshape((-1,) + (1,) * (len(extent) - 1 - position))
    return gain


def normal_values(stream_key, shape, width, limit, pieces=(), kind=jnp.bfloat16):
    drawn = jax.random.normal(stream_key, shape, jnp.float32) * width
    if len(pieces) > 0:
        drawn = level_of(stream_key, shape, pieces, -0.22, 0.18) * drawn
    return jnp.clip(drawn, min=-limit, max=limit).astype(kind)


def setup_inputs(seed: int = 0) -> dict:
    keys = jax.random.split(jax.random.key(seed), 11)
    return {
        "vectors": normal_values(keys[0], (ITEMS, NRHS), 1.0, 6.0, ((0, 64),)),
        "embeddings": draw_embeddings(jax.random.fold_in(keys[10], 71), 0),
        "basis": normal_values(keys[2], (ITEMS, RANK), LEAF ** -0.5, 0.75, ((0, 64),)),
        "transfer": normal_values(keys[3], (BOXES, RANK, RANK), (2 * RANK) ** -0.5, 0.5, ((0, 64),)),
        "coupling": normal_values(keys[4], (BLOCKS, RANK, RANK), (RANK * BLK_DEV * N_CPL // NODES_DEV) ** -0.5, 0.125, ((0, 256),)),
        "top_transfer": normal_values(keys[5], (TOPS, RANK, RANK), (2 * RANK) ** -0.5, 0.5),
        "top_coupling": normal_values(keys[6], (TOPS, RANK, RANK), (RANK // 16) ** -0.5, 3.0),
        "send_boxes": draw_send_boxes(jax.random.fold_in(keys[10], 71), 0),
        "block_slot": draw_block_slot(jax.random.fold_in(keys[10], 71), 0),
        "block_target": draw_block_target(jax.random.fold_in(keys[10], 71), 0),
    }


full_precision = lax.Precision.HIGHEST
sqrt_three = 1.7320508075688772

def matern_block(own_rows, other_rows):
    inner_products = jnp.einsum('bie,bje->bij', own_rows, other_rows, precision=full_precision)
    own_norms = lax.optimization_barrier(jnp.sum(own_rows * own_rows, axis=-1))
    other_norms = lax.optimization_barrier(jnp.sum(other_rows * other_rows, axis=-1))
    distance = jnp.sqrt(jnp.maximum(own_norms[:, :, None] + other_norms[:, None, :] - 2.0 * inner_products, 0.0))
    return ((1.0 + sqrt_three * distance) * jnp.exp(-sqrt_three * distance)).astype(jnp.bfloat16)

def reference(vectors, embeddings, basis, transfer, coupling, top_transfer, top_coupling, send_boxes, block_slot, block_target):
    leaf_vectors = vectors.reshape(LEAVES, LEAF, NRHS).astype(jnp.float32)
    leaf_basis = basis.reshape(LEAVES, LEAF, RANK).astype(jnp.float32)
    leaf_coef = jnp.einsum('bir,bin->brn', leaf_basis, leaf_vectors, precision=full_precision)
    matrices = transfer.astype(jnp.float32).reshape(N_LEAF, NODES_DEV, RANK, RANK)
    coef_levels = [leaf_coef.reshape(N_LEAF, B_DEV, RANK, NRHS)]
    for stratum in range(SUBL - 1, -1, -1):
        first_row = 2 ** (stratum + 1) - 1
        raised = jnp.einsum('pbrs,pbrn->pbsn', matrices[:, first_row:first_row + 2 ** (stratum + 1)], coef_levels[0], precision=full_precision)
        coef_levels.insert(0, raised[:, 0::2] + raised[:, 1::2])
    box_coef = jnp.concatenate(coef_levels, axis=1)
    root_up = jnp.einsum('prs,prn->psn', matrices[:, 0], box_coef[:, 0], precision=full_precision)
    top_matrices = top_transfer.astype(jnp.float32)
    top_couplings = top_coupling.astype(jnp.float32)
    top_coefs = {}
    raised = root_up
    for stratum in range(TOPL - 1, 0, -1):
        parents = raised[0::2] + raised[1::2]
        top_coefs[stratum] = parents
        if stratum > 1:
            first_row = 2 ** stratum - 2
            raised = jnp.einsum('brs,brn->bsn', top_matrices[first_row:first_row + 2 ** stratum], parents, precision=full_precision)
    top_down = None
    for stratum in range(1, TOPL):
        first_row = 2 ** stratum - 2
        count_here = 2 ** stratum
        siblings = top_coefs[stratum].reshape(count_here // 2, 2, RANK, NRHS)[:, ::-1].reshape(count_here, RANK, NRHS)
        fields = jnp.einsum('brs,bsn->brn', top_couplings[first_row:first_row + count_here], siblings, precision=full_precision)
        if top_down is None:
            top_down = fields
        else:
            top_down = fields + jnp.einsum('brs,bsn->brn', top_matrices[first_row:first_row + count_here], jnp.repeat(top_down, 2, axis=0), precision=full_precision)
    rounded = box_coef.astype(jnp.bfloat16).reshape(BOXES, RANK, NRHS)
    slot_boxes = send_boxes.reshape(N_LEAF, N_CPL, N_LEAF, CAP).transpose(2, 1, 0, 3).reshape(N_LEAF * N_CPL, SLOTS)
    sender_first = jnp.repeat(jnp.arange(N_LEAF, dtype=jnp.int32) * NODES_DEV, CAP)
    slot_global = (slot_boxes + sender_first[None, :]).astype(jnp.int32)

    def owner_fields(owner_args):
        owner_mats, owner_slots, owner_targets, owner_global = owner_args
        sources = jnp.take(rounded, jnp.take(owner_global, owner_slots), axis=0).astype(jnp.float32)
        products = jnp.einsum('brs,bsn->brn', owner_mats.astype(jnp.float32), sources, precision=full_precision)
        return jax.ops.segment_sum(products, owner_targets, num_segments=NODES_DEV + 1)[:NODES_DEV]
    partial_value = lax.map(owner_fields, (coupling.reshape(N_LEAF * N_CPL, BLK_DEV, RANK, RANK), block_slot.reshape(N_LEAF * N_CPL, BLK_DEV), block_target.reshape(N_LEAF * N_CPL, BLK_DEV), slot_global))
    list_field = lax.optimization_barrier(jnp.sum(partial_value.reshape(N_LEAF, N_CPL, NODES_DEV, RANK, NRHS), axis=1))
    parent_down = top_down[jnp.arange(N_LEAF, dtype=jnp.int32) // 2]
    current = list_field[:, 0:1] + jnp.einsum('prs,psn->prn', matrices[:, 0], parent_down, precision=full_precision)[:, None]
    for stratum in range(1, SUBL + 1):
        first_row = 2 ** stratum - 1
        current = list_field[:, first_row:first_row + 2 ** stratum] + jnp.einsum('pbrs,pbsn->pbrn', matrices[:, first_row:first_row + 2 ** stratum], jnp.repeat(current, 2, axis=1), precision=full_precision)
    leaf_down = lax.optimization_barrier(current.reshape(LEAVES, RANK, NRHS).astype(jnp.bfloat16)).astype(jnp.float32)
    far_part = jnp.einsum('bir,brn->bin', leaf_basis, leaf_down, precision=full_precision)
    leaf_embed = embeddings.reshape(LEAVES, LEAF, EMB).astype(jnp.float32)
    blank_embed = jnp.zeros((1, LEAF, EMB), jnp.float32)
    blank_vectors = jnp.zeros((1, LEAF, NRHS), jnp.float32)
    padded_embed = jnp.concatenate([blank_embed, leaf_embed, blank_embed], axis=0)
    padded_vectors = jnp.concatenate([blank_vectors, leaf_vectors, blank_vectors], axis=0)
    near_part = jnp.zeros((LEAVES, LEAF, NRHS), jnp.float32)
    for offset in range(3):
        kernel = lax.optimization_barrier(matern_block(leaf_embed, padded_embed[offset:offset + LEAVES])).astype(jnp.float32)
        near_part = near_part + jnp.einsum('bij,bjn->bin', kernel, padded_vectors[offset:offset + LEAVES], precision=full_precision)
    return (far_part + near_part).reshape(ITEMS, NRHS)
```

```python
import functools

import jax
import jax.numpy as jnp
from jax import lax
from jax.experimental import pallas as pl
from jax.experimental.pallas import tpu as pltpu
from jax.sharding import PartitionSpec as P

RANK = 64
NRHS = 64
LEAF = 64
B_DEV = 16
BOX = 2 * B_DEV - 1
BLK = 256
SHARE = 4
POS = 288
STEPS = POS // 2
PACK = 5

MESH = pl.DeviceIdType.MESH
f32, bf16, i32 = jnp.float32, jnp.bfloat16, jnp.int32
sqrt_three = 1.7320508075688772


def nn(a, b):
    return lax.dot_general(a, b, (((1,), (0,)), ((), ())), preferred_element_type=f32)


def nt(a, b):
    return lax.dot_general(a, b, (((1,), (1,)), ((), ())), preferred_element_type=f32)


def split_rows(x):
    upper = x.astype(bf16)
    lower = (x - upper.astype(f32)).astype(bf16)
    return jnp.concatenate([upper, lower], axis=0)


def wide(dot, x, w):
    rows = x.shape[0]
    y = dot(split_rows(x), w)
    return y[:rows] + y[rows:]


def lane_of(shape):
    return lax.broadcasted_iota(i32, shape, 1)


def row_of(shape):
    return lax.broadcasted_iota(i32, shape, 0)


def spread(tile):
    left = lane_of(tile.shape) < 64
    none = jnp.zeros_like(tile)
    return jnp.concatenate([jnp.where(left, tile, none), jnp.where(left, none, tile)], axis=0)


def kernel(
    n_leaf,
    vec_h, emb_h, bas_h, tra_h, cou_h, ttr_h, tco_h, send_boxes, slot_ref, target_ref,
    out_ref,
    vec, emb, bas, tra, cou, ttr, tco,
    left_box, right_box, outgoing, incoming, root_dup,
    top_out, top_in, top_coef, top_share, top_all,
    index_v, start_v, index_s, start_s,
    rows_f, blocks, prefix, field_f, field_b, field_in, near_ref,
    local_sem, halo_send, halo_recv, a2a_send, a2a_recv, top_send, top_recv,
    field_send, field_recv, down_send, down_recv,
):
    height = n_leaf.bit_length() - 1
    me = lax.axis_index("leaf")
    col = lax.axis_index("cpl")

    def peer(step):
        return lax.rem(me + step, n_leaf)

    def other(step):
        return lax.rem(col + step, SHARE)

    barrier = pltpu.get_barrier_semaphore()

    def greet(step, carry):
        pl.semaphore_signal(barrier, inc=1, device_id=(peer(step), col), device_id_type=MESH)
        return carry

    lax.fori_loop(1, n_leaf, greet, 0)
    for step in range(1, SHARE):
        pl.semaphore_signal(barrier, inc=1, device_id=(me, other(step)), device_id_type=MESH)

    loads = [
        pltpu.make_async_copy(vec_h, vec.at[:, pl.ds(128, 1024)], local_sem.at[0]),
        pltpu.make_async_copy(bas_h, bas, local_sem.at[1]),
        pltpu.make_async_copy(tra_h, tra, local_sem.at[2]),
        pltpu.make_async_copy(emb_h, emb.at[:, pl.ds(128, 1024)], local_sem.at[3]),
        pltpu.make_async_copy(cou_h, cou, local_sem.at[4]),
        pltpu.make_async_copy(ttr_h, ttr, local_sem.at[5]),
        pltpu.make_async_copy(tco_h, tco, local_sem.at[6]),
    ]
    for load in loads:
        load.start()

    loads[0].wait()
    loads[1].wait()
    tiles = []
    for j in range(B_DEV // 2):
        v = vec[:, 128 * (j + 1) : 128 * (j + 2)]
        tiles.append(nt(v, spread(bas[:, 128 * j : 128 * (j + 1)])))

    def keep_pair(first, tile):
        rounded = tile.astype(bf16)
        turned = pltpu.roll(rounded, 64, 1)
        left_box[first] = rounded
        right_box[first] = turned
        left_box[first + 1] = turned
        right_box[first + 1] = rounded

    loads[2].wait()
    first = B_DEV - 1
    for j, tile in enumerate(tiles):
        keep_pair(first + 2 * j, tile)
    while len(tiles) > 1:
        raised = []
        for j in range(len(tiles) // 2):
            w = tra[first + 4 * j : first + 4 * j + 4].reshape(256, 64)
            w = jnp.concatenate([w, w], axis=1)
            w = jnp.where((row_of(w.shape) < 128) == (lane_of(w.shape) < 64), w, jnp.zeros_like(w))
            raised.append(wide(nn, jnp.concatenate(tiles[2 * j : 2 * j + 2], axis=1), w))
        first = (first - 1) // 2
        tiles = raised
        for j, tile in enumerate(tiles):
            keep_pair(first + 2 * j, tile)
    w = tra[1:3].reshape(128, 64)
    root = wide(nn, tiles[0], jnp.concatenate([w, w], axis=1))
    left_box[0] = root.astype(bf16)
    right_box[0] = root.astype(bf16)

    pl.semaphore_wait(barrier, n_leaf - 1 + SHARE - 1)

    half = lane_of((64, 128)) < 64

    def a2a_copy(step):
        return pltpu.make_async_remote_copy(
            src_ref=outgoing.at[step],
            dst_ref=incoming.at[me],
            send_sem=a2a_send.at[step],
            recv_sem=a2a_recv.at[me],
            device_id=(peer(step), col),
            device_id_type=MESH,
        )

    def pick(d):
        return jnp.where(
            half, left_box[send_boxes[0, 0, 2 * d]], right_box[send_boxes[0, 0, 2 * d + 1]]
        )

    def give(i, carry):
        step = lax.rem((i // 2 + 1) * (1 - 2 * lax.rem(i, 2)) + n_leaf, n_leaf)
        outgoing[step] = pick(peer(step))
        a2a_copy(step).start()
        return carry

    lax.fori_loop(0, n_leaf - 1, give, 0)
    incoming[me] = pick(me)

    halos = []
    for k, (src_h, dst) in enumerate(((vec_h, vec), (emb_h, emb))):
        for side, (lanes, to, at) in enumerate(
            ((pl.ds(896, 128), peer(1), 0), (pl.ds(0, 128), peer(n_leaf - 1), 1152))
        ):
            halos.append(
                pltpu.make_async_remote_copy(
                    src_ref=src_h.at[:, lanes],
                    dst_ref=dst.at[:, pl.ds(at, 128)],
                    send_sem=halo_send.at[2 * k + side],
                    recv_sem=halo_recv.at[2 * k + side],
                    device_id=(to, col),
                    device_id_type=MESH,
                )
            )
            halos[-1].start()

    w = tra[0]
    root_dup[...] = wide(nn, root[:, :64], jnp.concatenate([w, w], axis=1))
    quarter = pl.multiple_of(col * 16, 16)
    half8 = lane_of((8, 128)) < 64
    top_out[...] = jnp.where(
        half8, root_dup[pl.ds(quarter, 8), :], root_dup[pl.ds(pl.multiple_of(quarter + 8, 8), 8), :]
    )

    def top_copy(step):
        return pltpu.make_async_remote_copy(
            src_ref=top_out,
            dst_ref=top_in.at[me],
            send_sem=top_send.at[step],
            recv_sem=top_recv.at[me],
            device_id=(peer(step), col),
            device_id_type=MESH,
        )

    def give_top(i, carry):
        step = lax.rem((i // 2 + 1) * (1 - 2 * lax.rem(i, 2)) + n_leaf, n_leaf)
        top_copy(step).start()
        return carry

    lax.fori_loop(0, n_leaf - 1, give_top, 0)
    top_in[me] = top_out[...]

    target = target_ref[...]
    slot = slot_ref[...]
    member = (target == row_of((32, BLK))).astype(f32)
    before = (row_of((BLK, BLK)) < lane_of((BLK, BLK))).astype(bf16)
    earlier = nn(member.astype(bf16), before)
    count = jnp.sum(member, axis=1, keepdims=True).astype(i32)
    even = ((count + 1) // 2) * 2
    even = jnp.where(row_of((32, 1)) < BOX, even, 0)
    below = (lane_of((32, 32)) < row_of((32, 32))).astype(bf16)
    start = nn(below, jnp.broadcast_to(even.astype(f32), (32, 128)).astype(bf16))
    start_v[...] = (start * 0.5).astype(i32)
    base = jnp.where(row_of((32, 1)) < BOX, start[:, :1], 4.0 * POS)
    rank = jnp.sum(member * (earlier + base), axis=0, keepdims=True).astype(i32)
    chosen = rank == row_of((POS, BLK))
    chosen_b = chosen.astype(bf16)
    pair_row = jnp.broadcast_to((slot // 2).astype(f32), (16, BLK)).astype(bf16)
    index_v[...] = nt(pair_row, chosen_b)[:8].astype(i32)
    odd = (slot - (slot // 2) * 2).astype(f32)
    odd_col = jnp.sum(jnp.where(chosen, odd, 0.0), axis=1, keepdims=True)
    half_f = (lane_of((POS, 128)) >= 64).astype(f32)
    used_half = (half_f == odd_col).astype(f32)
    copies = [
        pltpu.make_async_copy(index_v, index_s, local_sem.at[7]),
        pltpu.make_async_copy(start_v, start_s, local_sem.at[8]),
    ]
    for copy in copies:
        copy.start()

    loads[4].wait()

    def turn(r, carry):
        x, y = cou[r], cou[r + 32]
        d = nt(chosen_b, jnp.concatenate([x, x, y, y], axis=0))
        rows_f[pl.ds(r, POS, stride=64), :] = d[:, :128] * used_half
        rows_f[pl.ds(r + 32, POS, stride=64), :] = d[:, 128:] * used_half
        return carry

    lax.fori_loop(0, 32, turn, 0)

    def narrow(j, carry):
        blocks[j] = rows_f[pl.ds(pl.multiple_of(j * 64, 64), 64), :].astype(bf16)
        return carry

    lax.fori_loop(0, POS, narrow, 0)
    for copy in copies:
        copy.wait()

    loads[3].wait()
    for halo in halos:
        halo.wait()
    window = pl.ds(pl.multiple_of(col * 256, 256), 512)
    emb_t = emb[:, window]
    vec_t = vec[:, window]
    emb_w = emb_t.T
    squares = emb_w.astype(f32) * emb_w.astype(f32)
    norm_w = jnp.sum(squares, axis=1, keepdims=True)
    for a in range(2):
        own = emb_t[:, 128 * (a + 1) : 128 * (a + 2)]
        own_f = own.astype(f32)
        own_norm = jnp.sum(own_f * own_f, axis=0, keepdims=True)
        lo = 128 * a + 64
        inner = nn(emb_w[lo : lo + 256], own)
        distance = jnp.sqrt(jnp.maximum(norm_w[lo : lo + 256] + own_norm - 2.0 * inner, 0.0))
        scaled = sqrt_three * distance
        value = (1.0 + scaled) * jnp.exp(-scaled)
        row, lane = row_of((256, 128)), lane_of((256, 128))
        gap = row // 64 - lane // 64
        live = (gap >= 0) & (gap <= 2)
        if a == 0:
            live = live & ((row >= 64) | (me + col > 0))
        else:
            live = live & ((row < 192) | (me * SHARE + col < n_leaf * SHARE - 1))
        value = jnp.where(live, value, 0.0).astype(bf16)
        blank = jnp.zeros((64, 128), bf16)
        value = jnp.concatenate([blank, value, blank], axis=0)
        near_ref[:, 128 * a : 128 * (a + 1)] = nn(vec_t[:, 128 * a : 128 * a + 384], value)

    def arrived(step, carry):
        source = peer(step)
        pltpu.make_async_remote_copy(
            src_ref=outgoing.at[step],
            dst_ref=incoming.at[source],
            send_sem=a2a_send.at[step],
            recv_sem=a2a_recv.at[source],
            device_id=(source, col),
            device_id_type=MESH,
        ).wait()
        return carry

    lax.fori_loop(1, n_leaf, arrived, 0)

    prefix[0] = jnp.zeros((64, 64), f32)

    def from_pair(j):
        return jnp.clip(index_s[0, j], 0, n_leaf - 1)

    def couple(u, acc):
        source = jnp.concatenate(
            [incoming[from_pair(2 * u)], incoming[from_pair(2 * u + 1)]], axis=1
        )
        matrix = jnp.concatenate([blocks[2 * u], blocks[2 * u + 1]], axis=1)
        acc = acc + nt(source, matrix)
        prefix[u + 1] = acc
        return acc

    lax.fori_loop(0, STEPS, couple, jnp.zeros((64, 64), f32), unroll=4)

    def run(m):
        return jnp.clip(start_s[m, 0], 0, STEPS)

    def field(m):
        return prefix[run(m + 1)] - prefix[run(m)]

    def pair(a, b):
        return jnp.concatenate([field(a), field(b)], axis=1)

    for q in range(SHARE):
        packed = (
            pair(15 + 4 * q, 16 + 4 * q),
            pair(17 + 4 * q, 18 + 4 * q),
            pair(7 + 2 * q, 8 + 2 * q),
            pair(3 + q, 1 + q // 2),
            pair(0, 0),
        )
        for i, tile in enumerate(packed):
            field_f[q, i] = tile
            field_b[q, i] = tile.astype(bf16)

    def field_copy(step):
        return pltpu.make_async_remote_copy(
            src_ref=field_b.at[other(step)],
            dst_ref=field_in.at[col],
            send_sem=field_send.at[step],
            recv_sem=field_recv.at[col],
            device_id=(me, other(step)),
            device_id_type=MESH,
        )

    for step in range(1, SHARE):
        field_copy(step).start()

    loads[5].wait()
    loads[6].wait()

    def top_arrived(step, carry):
        source = peer(step)
        pltpu.make_async_remote_copy(
            src_ref=top_out,
            dst_ref=top_in.at[source],
            send_sem=top_send.at[step],
            recv_sem=top_recv.at[source],
            device_id=(source, col),
            device_id_type=MESH,
        ).wait()
        return carry

    lax.fori_loop(1, n_leaf, top_arrived, 0)
    for k in range(n_leaf // 2):
        both = top_in[2 * k] + top_in[2 * k + 1]
        top_coef[n_leaf // 2 + k] = jnp.concatenate([both[:, :64], both[:, 64:]], axis=0)
    for level in range(height - 2, 0, -1):
        for k in range(1 << level, 2 << level):
            children = jnp.concatenate([top_coef[2 * k], top_coef[2 * k + 1]], axis=1)
            top_coef[k] = wide(nn, children, ttr[2 * k - 2 : 2 * k].reshape(128, 64))
    down = None
    for level in range(1, height):
        node = (n_leaf + me) // (1 << (height - level))
        sibling = node + 1 - 2 * lax.rem(node, 2)
        here = wide(nt, top_coef[sibling], tco[node - 2])
        down = here if down is None else here + wide(nt, down, ttr[node - 2])
    top_share[...] = jnp.concatenate([down[:8], down[8:]], axis=1)

    def down_copy(step):
        return pltpu.make_async_remote_copy(
            src_ref=top_share,
            dst_ref=top_all.at[col],
            send_sem=down_send.at[step],
            recv_sem=down_recv.at[col],
            device_id=(me, other(step)),
            device_id_type=MESH,
        )

    for step in range(1, SHARE):
        down_copy(step).start()
    top_all[col] = top_share[...]

    def down_arrived(step):
        source = other(step)
        pltpu.make_async_remote_copy(
            src_ref=top_share,
            dst_ref=top_all.at[source],
            send_sem=down_send.at[step],
            recv_sem=down_recv.at[source],
            device_id=(me, source),
            device_id_type=MESH,
        ).wait()

    def field_arrived(step):
        source = other(step)
        pltpu.make_async_remote_copy(
            src_ref=field_b.at[source],
            dst_ref=field_in.at[source],
            send_sem=field_send.at[step],
            recv_sem=field_recv.at[source],
            device_id=(me, source),
            device_id_type=MESH,
        ).wait()

    for step in range(1, SHARE):
        field_arrived(step)
        down_arrived(step)

    def total(i):
        value = field_f[col, i]
        for step in range(1, SHARE):
            value = value + field_in[other(step), i].astype(f32)
        return value

    pieces = []
    for q in range(SHARE):
        tile = top_all[q]
        pieces += [tile[:, :64], tile[:, 64:]]
    parent = jnp.concatenate(pieces, axis=0)
    upper = total(3)
    down0 = total(4)[:, :64] + wide(nt, parent, tra[0])
    down1 = upper[:, 64:] + wide(nt, down0, tra[1 + col // 2])
    down2 = upper[:, :64] + wide(nt, down1, tra[3 + col])
    down3 = total(2) + wide(nt, down2, tra[pl.ds(7 + 2 * col, 2)].reshape(128, 64))
    for a in range(2):
        w = tra[pl.ds(15 + 4 * col + 2 * a, 2)].reshape(128, 64)
        leaf = total(a) + wide(nt, down3[:, 64 * a : 64 * (a + 1)], w)
        b = bas[:, pl.ds(pl.multiple_of(col * 256 + 128 * a, 128), 128)]
        out_ref[:, 128 * a : 128 * (a + 1)] = near_ref[:, 128 * a : 128 * (a + 1)] + nn(
            leaf.astype(bf16), spread(b)
        )


def body(
    vectors, embeddings, basis, transfer, coupling, top_transfer, top_coupling,
    send_boxes, block_slot, block_target,
):
    n_leaf = lax.axis_size("leaf")
    tops = top_transfer.shape[0]
    hbm = pl.BlockSpec(memory_space=pl.ANY)
    vmem = pl.BlockSpec(memory_space=pltpu.VMEM)
    smem = pl.BlockSpec(memory_space=pltpu.SMEM)
    dma = pltpu.SemaphoreType.DMA
    result = pl.pallas_call(
        functools.partial(kernel, n_leaf),
        out_shape=jax.ShapeDtypeStruct((NRHS, SHARE * LEAF), f32),
        in_specs=[hbm] * 7 + [smem, vmem, vmem],
        out_specs=vmem,
        scratch_shapes=[
            pltpu.VMEM((64, 1280), bf16),
            pltpu.VMEM((64, 1280), bf16),
            pltpu.VMEM((64, 1024), bf16),
            pltpu.VMEM((BOX, 64, 64), bf16),
            pltpu.VMEM((64, 64, BLK), bf16),
            pltpu.VMEM((tops, 64, 64), bf16),
            pltpu.VMEM((tops, 64, 64), bf16),
            pltpu.VMEM((BOX, 64, 128), bf16),
            pltpu.VMEM((BOX, 64, 128), bf16),
            pltpu.VMEM((n_leaf, 64, 128), bf16),
            pltpu.VMEM((n_leaf, 64, 128), bf16),
            pltpu.VMEM((64, 128), f32),
            pltpu.VMEM((8, 128), f32),
            pltpu.VMEM((n_leaf, 8, 128), f32),
            pltpu.VMEM((n_leaf, 16, 64), f32),
            pltpu.VMEM((8, 128), f32),
            pltpu.VMEM((SHARE, 8, 128), f32),
            pltpu.VMEM((8, POS), i32),
            pltpu.VMEM((32, 128), i32),
            pltpu.SMEM((8, POS), i32),
            pltpu.SMEM((32, 128), i32),
            pltpu.VMEM((POS * 64 + 64, 128), f32),
            pltpu.VMEM((POS, 64, 128), bf16),
            pltpu.VMEM((STEPS + 1, 64, 64), f32),
            pltpu.VMEM((SHARE, PACK, 64, 128), f32),
            pltpu.VMEM((SHARE, PACK, 64, 128), bf16),
            pltpu.VMEM((SHARE, PACK, 64, 128), bf16),
            pltpu.VMEM((64, SHARE * LEAF), f32),
            dma((9,)),
            dma((4,)),
            dma((4,)),
            dma((n_leaf,)),
            dma((n_leaf,)),
            dma((n_leaf,)),
            dma((n_leaf,)),
            dma((SHARE,)),
            dma((SHARE,)),
            dma((SHARE,)),
            dma((SHARE,)),
        ],
        compiler_params=pltpu.CompilerParams(
            collective_id=0, has_side_effects=True, vmem_limit_bytes=56 * 1024 * 1024
        ),
    )(
        vectors.T, embeddings.T, basis.T, transfer, jnp.transpose(coupling, (1, 2, 0)),
        top_transfer, top_coupling, send_boxes,
        block_slot.reshape(1, BLK), block_target.reshape(1, BLK),
    )
    return result.T


def solution(mesh):
    placed = (
        P("leaf", None),
        P("leaf", None),
        P("leaf", None),
        P("leaf", None, None),
        P(("leaf", "cpl"), None, None),
        P(),
        P(),
        P("leaf", "cpl", None),
        P(("leaf", "cpl")),
        P(("leaf", "cpl")),
    )
    return jax.shard_map(
        body, mesh=mesh, in_specs=placed, out_specs=P(("leaf", "cpl"), None), check_vma=False
    )
```

```python
import functools

import jax
import jax.numpy as jnp
from jax import lax
from jax.experimental import pallas as pl
from jax.experimental.pallas import tpu as pltpu
from jax.sharding import PartitionSpec as P

RANK = 64
NRHS = 64
LEAF = 64
B_DEV = 16
BOX = 2 * B_DEV - 1
BLK = 256
SHARE = 4
POS = 288
STEPS = POS // 2
GROUP = 16

MESH = pl.DeviceIdType.MESH
f32, bf16, i32 = jnp.float32, jnp.bfloat16, jnp.int32
sqrt_three = 1.7320508075688772


def nn(a, b):
    return lax.dot_general(a, b, (((1,), (0,)), ((), ())), preferred_element_type=f32)


def nt(a, b):
    return lax.dot_general(a, b, (((1,), (1,)), ((), ())), preferred_element_type=f32)


def split_rows(x):
    upper = x.astype(bf16)
    lower = (x - upper.astype(f32)).astype(bf16)
    return jnp.concatenate([upper, lower], axis=0)


def wide(dot, x, w):
    rows = x.shape[0]
    y = dot(split_rows(x), w)
    return y[:rows] + y[rows:]


def lane_of(shape):
    return lax.broadcasted_iota(i32, shape, 1)


def row_of(shape):
    return lax.broadcasted_iota(i32, shape, 0)


def spread(tile):
    left = lane_of(tile.shape) < 64
    none = jnp.zeros_like(tile)
    return jnp.concatenate([jnp.where(left, tile, none), jnp.where(left, none, tile)], axis=0)


def kernel(
    n_leaf,
    vec_h, emb_h, bas_h, tra_h, cou_h, ttr_h, tco_h, send_boxes, slot_ref, target_ref,
    out_ref,
    vec, emb, bas, tra, cou, ttr, tco,
    left_box, right_box, outgoing, incoming, root_dup,
    lifts, top_out, top_in, group_coef, group_out, group_in, upper_coef, top_share, top_all,
    index_v, start_v, index_s, start_s,
    rows_f, blocks, prefix, leaf_f, leaf_b, leaf_in, near_ref,
    local_sem, halo_send, halo_recv, a2a_send, a2a_recv, top_send, top_recv,
    group_send, group_recv, field_send, field_recv, down_send, down_recv,
):
    height = n_leaf.bit_length() - 1
    me = lax.axis_index("leaf")
    col = lax.axis_index("cpl")

    def peer(step):
        return lax.rem(me + step, n_leaf)

    def other(step):
        return lax.rem(col + step, SHARE)

    barrier = pltpu.get_barrier_semaphore()

    def greet(step, carry):
        pl.semaphore_signal(barrier, inc=1, device_id=(peer(step), col), device_id_type=MESH)
        return carry

    lax.fori_loop(1, n_leaf, greet, 0)
    for step in range(1, SHARE):
        pl.semaphore_signal(barrier, inc=1, device_id=(me, other(step)), device_id_type=MESH)

    loads = [
        pltpu.make_async_copy(vec_h, vec.at[:, pl.ds(128, 1024)], local_sem.at[0]),
        pltpu.make_async_copy(bas_h, bas, local_sem.at[1]),
        pltpu.make_async_copy(tra_h, tra, local_sem.at[2]),
        pltpu.make_async_copy(emb_h, emb.at[:, pl.ds(128, 1024)], local_sem.at[3]),
        pltpu.make_async_copy(cou_h, cou, local_sem.at[4]),
        pltpu.make_async_copy(ttr_h, ttr, local_sem.at[5]),
        pltpu.make_async_copy(tco_h, tco, local_sem.at[6]),
    ]
    for load in loads:
        load.start()

    loads[0].wait()
    loads[1].wait()
    tiles = []
    for j in range(B_DEV // 2):
        v = vec[:, 128 * (j + 1) : 128 * (j + 2)]
        tiles.append(nt(v, spread(bas[:, 128 * j : 128 * (j + 1)])))

    def keep_pair(first, tile):
        rounded = tile.astype(bf16)
        turned = pltpu.roll(rounded, 64, 1)
        left_box[first] = rounded
        right_box[first] = turned
        left_box[first + 1] = turned
        right_box[first + 1] = rounded

    loads[2].wait()
    first = B_DEV - 1
    for j, tile in enumerate(tiles):
        keep_pair(first + 2 * j, tile)
    while len(tiles) > 1:
        raised = []
        for j in range(len(tiles) // 2):
            w = tra[first + 4 * j : first + 4 * j + 4].reshape(256, 64)
            w = jnp.concatenate([w, w], axis=1)
            w = jnp.where((row_of(w.shape) < 128) == (lane_of(w.shape) < 64), w, jnp.zeros_like(w))
            lifts[len(tiles) // 2 - 1 + j] = w
            raised.append(wide(nn, jnp.concatenate(tiles[2 * j : 2 * j + 2], axis=1), w))
        first = (first - 1) // 2
        tiles = raised
        for j, tile in enumerate(tiles):
            keep_pair(first + 2 * j, tile)
    w = tra[1:3].reshape(128, 64)
    root = wide(nn, tiles[0], jnp.concatenate([w, w], axis=1))
    left_box[0] = root.astype(bf16)
    right_box[0] = root.astype(bf16)

    pl.semaphore_wait(barrier, n_leaf - 1 + SHARE - 1)

    group = me // GROUP
    groups = n_leaf // GROUP
    inside = lax.rem(me, GROUP)
    w = tra[0]
    root_dup[...] = wide(nn, root[:, :64], jnp.concatenate([w, w], axis=1))
    quarter = pl.multiple_of(col * 16, 16)
    half8 = lane_of((8, 128)) < 64
    top_out[...] = jnp.where(
        half8, root_dup[pl.ds(quarter, 8), :], root_dup[pl.ds(pl.multiple_of(quarter + 8, 8), 8), :]
    )

    def mate(step):
        return lax.rem(inside + step, GROUP)

    def top_copy(step, source):
        return pltpu.make_async_remote_copy(
            src_ref=top_out,
            dst_ref=top_in.at[source],
            send_sem=top_send.at[step],
            recv_sem=top_recv.at[source],
            device_id=(group * GROUP + mate(step), col),
            device_id_type=MESH,
        )

    def group_copy(step, source):
        return pltpu.make_async_remote_copy(
            src_ref=group_out,
            dst_ref=group_in.at[source],
            send_sem=group_send.at[step],
            recv_sem=group_recv.at[source],
            device_id=(lax.rem(group + step, groups) * GROUP + inside, col),
            device_id_type=MESH,
        )

    for step in range(1, GROUP):
        top_copy(step, inside).start()
    top_in[inside] = top_out[...]

    half = lane_of((64, 128)) < 64

    def a2a_copy(step):
        return pltpu.make_async_remote_copy(
            src_ref=outgoing.at[step],
            dst_ref=incoming.at[me],
            send_sem=a2a_send.at[step],
            recv_sem=a2a_recv.at[me],
            device_id=(peer(step), col),
            device_id_type=MESH,
        )

    def pick(d):
        return jnp.where(
            half, left_box[send_boxes[0, 0, 2 * d]], right_box[send_boxes[0, 0, 2 * d + 1]]
        )

    def give(i, carry):
        step = lax.rem((i // 2 + 1) * (1 - 2 * lax.rem(i, 2)) + n_leaf, n_leaf)
        outgoing[step] = pick(peer(step))
        a2a_copy(step).start()
        return carry

    lax.fori_loop(0, n_leaf - 1, give, 0)
    incoming[me] = pick(me)

    halos = []
    for k, (src_h, dst) in enumerate(((vec_h, vec), (emb_h, emb))):
        for side, (lanes, to, at) in enumerate(
            ((pl.ds(896, 128), peer(1), 0), (pl.ds(0, 128), peer(n_leaf - 1), 1152))
        ):
            halos.append(
                pltpu.make_async_remote_copy(
                    src_ref=src_h.at[:, lanes],
                    dst_ref=dst.at[:, pl.ds(at, 128)],
                    send_sem=halo_send.at[2 * k + side],
                    recv_sem=halo_recv.at[2 * k + side],
                    device_id=(to, col),
                    device_id_type=MESH,
                )
            )
            halos[-1].start()

    target = target_ref[...]
    slot = slot_ref[...]
    member = (target == row_of((32, BLK))).astype(f32)
    before = (row_of((BLK, BLK)) < lane_of((BLK, BLK))).astype(bf16)
    earlier = nn(member.astype(bf16), before)
    count = jnp.sum(member, axis=1, keepdims=True).astype(i32)
    even = ((count + 1) // 2) * 2
    even = jnp.where(row_of((32, 1)) < BOX, even, 0)
    below = (lane_of((32, 32)) < row_of((32, 32))).astype(bf16)
    start = nn(below, jnp.broadcast_to(even.astype(f32), (32, 128)).astype(bf16))
    start_v[...] = (start * 0.5).astype(i32)
    base = jnp.where(row_of((32, 1)) < BOX, start[:, :1], 4.0 * POS)
    rank = jnp.sum(member * (earlier + base), axis=0, keepdims=True).astype(i32)
    chosen = rank == row_of((POS, BLK))
    chosen_b = chosen.astype(bf16)
    pair_row = jnp.broadcast_to((slot // 2).astype(f32), (16, BLK)).astype(bf16)
    index_v[...] = nt(pair_row, chosen_b)[:8].astype(i32)
    odd = (slot - (slot // 2) * 2).astype(f32)
    odd_col = jnp.sum(jnp.where(chosen, odd, 0.0), axis=1, keepdims=True)
    half_f = (lane_of((POS, 128)) >= 64).astype(f32)
    used_half = (half_f == odd_col).astype(f32)
    copies = [
        pltpu.make_async_copy(index_v, index_s, local_sem.at[7]),
        pltpu.make_async_copy(start_v, start_s, local_sem.at[8]),
    ]
    for copy in copies:
        copy.start()

    def unpack(tile):
        return jnp.concatenate([tile[:, :64], tile[:, 64:]], axis=0)

    def pack(value):
        return jnp.concatenate([value[:8], value[8:]], axis=1)

    loads[5].wait()
    loads[6].wait()
    for step in range(1, GROUP):
        top_copy(step, mate(step)).wait()
    depth = GROUP.bit_length() - 1
    for k in range(GROUP // 2):
        group_coef[GROUP // 2 + k] = unpack(top_in[2 * k] + top_in[2 * k + 1])
    for level in range(depth - 2, -1, -1):
        for k in range(1 << level):
            child = 2 * ((1 << level) + k)
            children = jnp.concatenate([group_coef[child], group_coef[child + 1]], axis=1)
            matrix = ttr[pl.ds(((groups + group) << (level + 1)) + 2 * k - 2, 2)].reshape(128, 64)
            group_coef[(1 << level) + k] = wide(nn, children, matrix)
    group_out[...] = pack(group_coef[1])
    for step in range(1, groups):
        group_copy(step, group).start()
    group_in[group] = group_out[...]

    loads[4].wait()

    def turn(r, carry):
        x, y = cou[r], cou[r + 32]
        d = nt(chosen_b, jnp.concatenate([x, x, y, y], axis=0))
        rows_f[pl.ds(r, POS, stride=64), :] = d[:, :128] * used_half
        rows_f[pl.ds(r + 32, POS, stride=64), :] = d[:, 128:] * used_half
        return carry

    lax.fori_loop(0, 32, turn, 0, unroll=4)

    for step in range(1, groups):
        group_copy(step, lax.rem(group + step, groups)).wait()
    for k in range(groups):
        upper_coef[groups + k] = unpack(group_in[k])
    for k in range(groups - 1, 1, -1):
        children = jnp.concatenate([upper_coef[2 * k], upper_coef[2 * k + 1]], axis=1)
        upper_coef[k] = wide(nn, children, ttr[2 * k - 2 : 2 * k].reshape(128, 64))
    down = None
    for level in range(1, height):
        node = (n_leaf + me) // (1 << (height - level))
        sibling = node + 1 - 2 * lax.rem(node, 2)
        below = level - (groups.bit_length() - 1)
        if below <= 0:
            beside = upper_coef[sibling]
        else:
            beside = group_coef[sibling - ((groups + group) << below) + (1 << below)]
        here = wide(nt, beside, tco[node - 2])
        down = here if down is None else here + wide(nt, down, ttr[node - 2])
    top_share[...] = pack(down)

    def down_copy(step, source):
        return pltpu.make_async_remote_copy(
            src_ref=top_share,
            dst_ref=top_all.at[source],
            send_sem=down_send.at[step],
            recv_sem=down_recv.at[source],
            device_id=(me, other(step)),
            device_id_type=MESH,
        )

    for step in range(1, SHARE):
        down_copy(step, col).start()
    top_all[col] = top_share[...]

    def narrow(j, carry):
        blocks[j] = rows_f[pl.ds(pl.multiple_of(j * 64, 64), 64), :].astype(bf16)
        return carry

    lax.fori_loop(0, POS, narrow, 0, unroll=8)
    for copy in copies:
        copy.wait()

    loads[3].wait()
    for halo in halos:
        halo.wait()
    window = pl.ds(pl.multiple_of(col * 256, 256), 512)
    emb_t = emb[:, window]
    vec_t = vec[:, window]
    emb_w = emb_t.T
    squares = emb_w.astype(f32) * emb_w.astype(f32)
    norm_w = jnp.sum(squares, axis=1, keepdims=True)
    for a in range(2):
        own = emb_t[:, 128 * (a + 1) : 128 * (a + 2)]
        own_f = own.astype(f32)
        own_norm = jnp.sum(own_f * own_f, axis=0, keepdims=True)
        lo = 128 * a + 64
        inner = nn(emb_w[lo : lo + 256], own)
        distance = jnp.sqrt(jnp.maximum(norm_w[lo : lo + 256] + own_norm - 2.0 * inner, 0.0))
        scaled = sqrt_three * distance
        value = (1.0 + scaled) * jnp.exp(-scaled)
        row, lane = row_of((256, 128)), lane_of((256, 128))
        gap = row // 64 - lane // 64
        live = (gap >= 0) & (gap <= 2)
        if a == 0:
            live = live & ((row >= 64) | (me + col > 0))
        else:
            live = live & ((row < 192) | (me * SHARE + col < n_leaf * SHARE - 1))
        value = jnp.where(live, value, 0.0).astype(bf16)
        blank = jnp.zeros((64, 128), bf16)
        value = jnp.concatenate([blank, value, blank], axis=0)
        near_ref[:, 128 * a : 128 * (a + 1)] = nn(vec_t[:, 128 * a : 128 * a + 384], value)

    for step in range(1, SHARE):
        down_copy(step, other(step)).wait()
    parent = jnp.concatenate([unpack(top_all[q]) for q in range(SHARE)], axis=0)
    parent = wide(nt, parent, tra[0])
    parent = wide(nt, parent, tra[1 + col // 2])
    parent = wide(nt, parent, tra[3 + col])
    parent = wide(nt, parent, tra[pl.ds(7 + 2 * col, 2)].reshape(128, 64))
    from_top = []
    for a in range(2):
        w = tra[pl.ds(15 + 4 * col + 2 * a, 2)].reshape(128, 64)
        from_top.append(wide(nt, parent[:, 64 * a : 64 * (a + 1)], w))

    def arrived(step, carry):
        source = peer(step)
        pltpu.make_async_remote_copy(
            src_ref=outgoing.at[step],
            dst_ref=incoming.at[source],
            send_sem=a2a_send.at[step],
            recv_sem=a2a_recv.at[source],
            device_id=(source, col),
            device_id_type=MESH,
        ).wait()
        return carry

    lax.fori_loop(1, n_leaf, arrived, 0)

    prefix[0] = jnp.zeros((64, 64), f32)

    def from_pair(j):
        return jnp.clip(index_s[0, j], 0, n_leaf - 1)

    def couple(u, acc):
        source = jnp.concatenate(
            [incoming[from_pair(2 * u)], incoming[from_pair(2 * u + 1)]], axis=1
        )
        matrix = jnp.concatenate([blocks[2 * u], blocks[2 * u + 1]], axis=1)
        acc = acc + nt(source, matrix)
        prefix[u + 1] = acc
        return acc

    lax.fori_loop(0, STEPS, couple, jnp.zeros((64, 64), f32), unroll=48)

    def run(m):
        return jnp.clip(start_s[m, 0], 0, STEPS)

    def field(m):
        return prefix[run(m + 1)] - prefix[run(m)]

    def pair(a, b):
        return jnp.concatenate([field(a), field(b)], axis=1)

    line = pair(1, 2) + wide(nt, field(0), tra[1:3].reshape(128, 64))
    lines = [line]
    for level in range(2, 5):
        first = (1 << level) - 1
        lower = []
        for j, tile in enumerate(lines):
            both = wide(nt, tile, lifts[len(lines) - 1 + j])
            lower.append(pair(first + 4 * j, first + 4 * j + 1) + both[:, :128])
            lower.append(pair(first + 4 * j + 2, first + 4 * j + 3) + both[:, 128:])
        lines = lower
    for j, tile in enumerate(lines):
        leaf_f[j] = tile
        leaf_b[j] = tile.astype(bf16)

    def field_copy(step, source):
        return pltpu.make_async_remote_copy(
            src_ref=leaf_b.at[pl.ds(2 * other(step), 2)],
            dst_ref=leaf_in.at[source],
            send_sem=field_send.at[step],
            recv_sem=field_recv.at[source],
            device_id=(me, other(step)),
            device_id_type=MESH,
        )

    for step in range(1, SHARE):
        field_copy(step, col).start()
    for step in range(1, SHARE):
        field_copy(step, other(step)).wait()

    for a in range(2):
        leaf = leaf_f[2 * col + a] + from_top[a]
        for step in range(1, SHARE):
            leaf = leaf + leaf_in[other(step), a].astype(f32)
        b = bas[:, pl.ds(pl.multiple_of(col * 256 + 128 * a, 128), 128)]
        out_ref[:, 128 * a : 128 * (a + 1)] = near_ref[:, 128 * a : 128 * (a + 1)] + nn(
            leaf.astype(bf16), spread(b)
        )


def body(
    vectors, embeddings, basis, transfer, coupling, top_transfer, top_coupling,
    send_boxes, block_slot, block_target,
):
    n_leaf = lax.axis_size("leaf")
    tops = top_transfer.shape[0]
    hbm = pl.BlockSpec(memory_space=pl.ANY)
    vmem = pl.BlockSpec(memory_space=pltpu.VMEM)
    smem = pl.BlockSpec(memory_space=pltpu.SMEM)
    dma = pltpu.SemaphoreType.DMA
    result = pl.pallas_call(
        functools.partial(kernel, n_leaf),
        out_shape=jax.ShapeDtypeStruct((NRHS, SHARE * LEAF), f32),
        in_specs=[hbm] * 7 + [smem, vmem, vmem],
        out_specs=vmem,
        scratch_shapes=[
            pltpu.VMEM((64, 1280), bf16),
            pltpu.VMEM((64, 1280), bf16),
            pltpu.VMEM((64, 1024), bf16),
            pltpu.VMEM((BOX, 64, 64), bf16),
            pltpu.VMEM((64, 64, BLK), bf16),
            pltpu.VMEM((tops, 64, 64), bf16),
            pltpu.VMEM((tops, 64, 64), bf16),
            pltpu.VMEM((BOX, 64, 128), bf16),
            pltpu.VMEM((BOX, 64, 128), bf16),
            pltpu.VMEM((n_leaf, 64, 128), bf16),
            pltpu.VMEM((n_leaf, 64, 128), bf16),
            pltpu.VMEM((64, 128), f32),
            pltpu.VMEM((7, 256, 128), bf16),
            pltpu.VMEM((8, 128), f32),
            pltpu.VMEM((GROUP, 8, 128), f32),
            pltpu.VMEM((GROUP, 16, 64), f32),
            pltpu.VMEM((8, 128), f32),
            pltpu.VMEM((n_leaf // GROUP, 8, 128), f32),
            pltpu.VMEM((2 * n_leaf // GROUP, 16, 64), f32),
            pltpu.VMEM((8, 128), f32),
            pltpu.VMEM((SHARE, 8, 128), f32),
            pltpu.VMEM((8, POS), i32),
            pltpu.VMEM((32, 128), i32),
            pltpu.SMEM((8, POS), i32),
            pltpu.SMEM((32, 128), i32),
            pltpu.VMEM((POS * 64 + 64, 128), f32),
            pltpu.VMEM((POS, 64, 128), bf16),
            pltpu.VMEM((STEPS + 1, 64, 64), f32),
            pltpu.VMEM((B_DEV // 2, 64, 128), f32),
            pltpu.VMEM((B_DEV // 2, 64, 128), bf16),
            pltpu.VMEM((SHARE, 2, 64, 128), bf16),
            pltpu.VMEM((64, SHARE * LEAF), f32),
            dma((9,)),
            dma((4,)),
            dma((4,)),
            dma((n_leaf,)),
            dma((n_leaf,)),
            dma((GROUP,)),
            dma((GROUP,)),
            dma((n_leaf // GROUP,)),
            dma((n_leaf // GROUP,)),
            dma((SHARE,)),
            dma((SHARE,)),
            dma((SHARE,)),
            dma((SHARE,)),
        ],
        compiler_params=pltpu.CompilerParams(
            collective_id=0, has_side_effects=True, vmem_limit_bytes=56 * 1024 * 1024
        ),
    )(
        vectors.T, embeddings.T, basis.T, transfer, jnp.transpose(coupling, (1, 2, 0)),
        top_transfer, top_coupling, send_boxes,
        block_slot.reshape(1, BLK), block_target.reshape(1, BLK),
    )
    return result.T


def solution(mesh):
    placed = (
        P("leaf", None),
        P("leaf", None),
        P("leaf", None),
        P("leaf", None, None),
        P(("leaf", "cpl"), None, None),
        P(),
        P(),
        P("leaf", "cpl", None),
        P(("leaf", "cpl")),
        P(("leaf", "cpl")),
    )
    return jax.shard_map(
        body, mesh=mesh, in_specs=placed, out_specs=P(("leaf", "cpl"), None), check_vma=False
    )
```

```python
import functools

import jax
import jax.numpy as jnp
from jax import lax
from jax.experimental import pallas as pl
from jax.experimental.pallas import tpu as pltpu
from jax.sharding import PartitionSpec as P

RANK = 64
NRHS = 64
LEAF = 64
B_DEV = 16
BOX = 2 * B_DEV - 1
BLK = 256
SHARE = 4
POS = 288
STEPS = POS // 2
GROUP = 16

MESH = pl.DeviceIdType.MESH
f32, bf16, i32 = jnp.float32, jnp.bfloat16, jnp.int32
sqrt_three = 1.7320508075688772


def nn(a, b):
    return lax.dot_general(a, b, (((1,), (0,)), ((), ())), preferred_element_type=f32)


def nt(a, b):
    return lax.dot_general(a, b, (((1,), (1,)), ((), ())), preferred_element_type=f32)


def split_rows(x):
    upper = x.astype(bf16)
    lower = (x - upper.astype(f32)).astype(bf16)
    return jnp.concatenate([upper, lower], axis=0)


def wide(dot, x, w):
    rows = x.shape[0]
    y = dot(split_rows(x), w)
    return y[:rows] + y[rows:]


def lane_of(shape):
    return lax.broadcasted_iota(i32, shape, 1)


def row_of(shape):
    return lax.broadcasted_iota(i32, shape, 0)


def spread(tile):
    left = lane_of(tile.shape) < 64
    none = jnp.zeros_like(tile)
    return jnp.concatenate([jnp.where(left, tile, none), jnp.where(left, none, tile)], axis=0)


def kernel(
    n_leaf,
    vec_h, emb_h, bas_h, tra_h, cou_h, ttr_h, tco_h, send_boxes, slot_ref, target_ref,
    out_ref,
    vec, emb, bas, tra, cou, ttr, tco,
    tiles_out, shares, choice, outgoing, incoming, root_dup, plan_own, plan_in, plan_v, plan_s,
    lifts, top_out, top_in, group_coef, group_out, group_in, upper_coef, top_share, top_all,
    index_v, start_v, index_s, start_s,
    rows_f, blocks, prefix, leaf_f, leaf_b, leaf_in, near_ref,
    local_sem, halo_send, halo_recv, plan_send, plan_recv, ring_send, ring_recv,
    a2a_send, a2a_recv, top_send, top_recv,
    group_send, group_recv, field_send, field_recv, down_send, down_recv,
):
    height = n_leaf.bit_length() - 1
    me = lax.axis_index("leaf")
    col = lax.axis_index("cpl")

    group = me // GROUP
    groups = n_leaf // GROUP
    inside = lax.rem(me, GROUP)
    depth_z = GROUP // 2
    plane = 2 * groups * SHARE
    z = inside // 2
    core = lax.rem(inside, 2)

    def leaf_at(x, z_at, c):
        return x * GROUP + z_at * 2 + c

    def other(step):
        return lax.rem(col + step, SHARE)

    def mate(step):
        return lax.rem(inside + step, GROUP)

    def in_plane(r):
        return (
            lax.rem(group + r // (2 * SHARE), groups),
            lax.rem(core + lax.rem(r // SHARE, 2), 2),
            other(lax.rem(r, SHARE)),
        )

    def in_column(r):
        return lax.rem(z + r // SHARE, depth_z), other(lax.rem(r, SHARE))

    next_leaf = lax.rem(me + 1, n_leaf)
    last_leaf = lax.rem(me + n_leaf - 1, n_leaf)

    loads = [
        pltpu.make_async_copy(vec_h, vec.at[:, pl.ds(128, 1024)], local_sem.at[0]),
        pltpu.make_async_copy(bas_h, bas, local_sem.at[1]),
        pltpu.make_async_copy(tra_h, tra, local_sem.at[2]),
        pltpu.make_async_copy(emb_h, emb.at[:, pl.ds(128, 1024)], local_sem.at[3]),
        pltpu.make_async_copy(cou_h, cou, local_sem.at[4]),
        pltpu.make_async_copy(ttr_h, ttr, local_sem.at[5]),
        pltpu.make_async_copy(tco_h, tco, local_sem.at[6]),
    ]
    for load in loads[:3]:
        load.start()

    barrier = pltpu.get_barrier_semaphore()

    def greet(leaf, cpl):
        pl.semaphore_signal(barrier, inc=1, device_id=(leaf, cpl), device_id_type=MESH)

    def greet_plane(r, carry):
        x_at, core_at, cpl_at = in_plane(r)
        greet(leaf_at(x_at, z, core_at), cpl_at)
        return carry

    def greet_column(r, carry):
        z_at, cpl_at = in_column(r)
        greet(leaf_at(group, z_at, core), cpl_at)
        return carry

    def greet_mate(step, carry):
        greet(group * GROUP + mate(step), col)
        return carry

    lax.fori_loop(1, plane, greet_plane, 0)
    lax.fori_loop(SHARE, depth_z * SHARE, greet_column, 0)
    lax.fori_loop(1, GROUP, greet_mate, 0)
    greet(next_leaf, col)
    greet(last_leaf, col)
    greetings = plane - 1 + (depth_z - 1) * SHARE + GROUP - 1 + 2

    loads[0].wait()
    loads[1].wait()
    tiles = []
    for j in range(B_DEV // 2):
        v = vec[:, 128 * (j + 1) : 128 * (j + 2)]
        tiles.append(nt(v, spread(bas[:, 128 * j : 128 * (j + 1)])))

    def keep_pair(first, tile):
        tiles_out[(first + 1) // 2] = tile.astype(bf16)

    first = B_DEV - 1
    for j, tile in enumerate(tiles):
        keep_pair(first + 2 * j, tile)
    loads[2].wait()
    for load in loads[3:]:
        load.start()

    pl.semaphore_wait(barrier, greetings)

    quarter = pl.multiple_of(col * 16, 16)

    def ring_copy(hop, way, tiles_at, source, src):
        return pltpu.make_async_remote_copy(
            src_ref=src,
            dst_ref=shares.at[source, tiles_at],
            send_sem=ring_send.at[way, hop],
            recv_sem=ring_recv.at[source],
            device_id=(leaf_at(group, lax.rem(z + (1, depth_z - 1)[way], depth_z), core), col),
            device_id_type=MESH,
        )

    hops = (depth_z // 2, depth_z // 2 - 1)

    def ring_own(tiles_at):
        for way in range(2):
            if hops[way] > 0:
                ring_copy(
                    0, way, tiles_at, z, tiles_out.at[tiles_at, pl.ds(quarter, 16)]
                ).start()

    ring_own(pl.ds(8, 8))

    plan_own[...] = send_boxes[0]

    def plan_copy(r, z_at, cpl_at):
        z_to, cpl_to = in_column(r)
        return pltpu.make_async_remote_copy(
            src_ref=plan_own,
            dst_ref=plan_in.at[cpl_at, pl.ds(z_at, 1)],
            send_sem=plan_send.at[r],
            recv_sem=plan_recv.at[cpl_at * depth_z + z_at],
            device_id=(leaf_at(group, z_to, core), cpl_to),
            device_id_type=MESH,
        )

    def give_plan(r, carry):
        plan_copy(r, z, col).start()
        return carry

    lax.fori_loop(1, depth_z * SHARE, give_plan, 0)
    plan_in[col, pl.ds(z, 1)] = plan_own[...]

    while len(tiles) > 1:
        raised = []
        for j in range(len(tiles) // 2):
            w = tra[first + 4 * j : first + 4 * j + 4].reshape(256, 64)
            w = jnp.concatenate([w, w], axis=1)
            w = jnp.where((row_of(w.shape) < 128) == (lane_of(w.shape) < 64), w, jnp.zeros_like(w))
            lifts[len(tiles) // 2 - 1 + j] = w
            raised.append(wide(nn, jnp.concatenate(tiles[2 * j : 2 * j + 2], axis=1), w))
        first = (first - 1) // 2
        tiles = raised
        for j, tile in enumerate(tiles):
            keep_pair(first + 2 * j, tile)
    w = tra[1:3].reshape(128, 64)
    root = wide(nn, tiles[0], jnp.concatenate([w, w], axis=1))
    tiles_out[0] = root.astype(bf16)
    ring_own(pl.ds(0, 8))
    shares[z] = tiles_out[:, pl.ds(quarter, 16)]

    w = tra[0]
    root_dup[...] = wide(nn, root[:, :64], jnp.concatenate([w, w], axis=1))
    half8 = lane_of((8, 128)) < 64
    top_out[...] = jnp.where(
        half8, root_dup[pl.ds(quarter, 8), :], root_dup[pl.ds(pl.multiple_of(quarter + 8, 8), 8), :]
    )

    def top_copy(step, source):
        return pltpu.make_async_remote_copy(
            src_ref=top_out,
            dst_ref=top_in.at[source],
            send_sem=top_send.at[step],
            recv_sem=top_recv.at[source],
            device_id=(group * GROUP + mate(step), col),
            device_id_type=MESH,
        )

    def group_copy(step, source):
        return pltpu.make_async_remote_copy(
            src_ref=group_out,
            dst_ref=group_in.at[source],
            send_sem=group_send.at[step],
            recv_sem=group_recv.at[source],
            device_id=(lax.rem(group + step, groups) * GROUP + inside, col),
            device_id_type=MESH,
        )

    for step in range(1, GROUP):
        top_copy(step, inside).start()
    top_in[inside] = top_out[...]

    halos = []
    for k, (src_h, dst) in enumerate(((vec_h, vec), (emb_h, emb))):
        for side, (lanes, to, at) in enumerate(
            ((pl.ds(896, 128), next_leaf, 0), (pl.ds(0, 128), last_leaf, 1152))
        ):
            halos.append(
                pltpu.make_async_remote_copy(
                    src_ref=src_h.at[:, lanes],
                    dst_ref=dst.at[:, pl.ds(at, 128)],
                    send_sem=halo_send.at[2 * k + side],
                    recv_sem=halo_recv.at[2 * k + side],
                    device_id=(to, col),
                    device_id_type=MESH,
                )
            )
            halos[-1].start()

    def plan_wait(r, carry):
        z_at, cpl_at = in_column(r)
        plan_copy(r, z_at, cpl_at).wait()
        return carry

    lax.fori_loop(1, depth_z * SHARE, plan_wait, 0)
    box = plan_in[...].reshape(SHARE * depth_z, 2 * n_leaf)
    even_box = box - (box // 2) * 2 == 0
    even_slot = lax.rem(lane_of(box.shape), 2) == 0
    plan_v[...] = (box + 1) // 2 + jnp.where(even_box == even_slot, 16, 0)
    plan_done = pltpu.make_async_copy(plan_v, plan_s, local_sem.at[9])
    plan_done.start()
    half = lane_of((16, 128)) < 64

    def take(row, lane):
        return plan_s[row, lane]

    def give(source):
        whole = shares[source].reshape(256, 128)
        choice[0:16] = whole.reshape(16, 16, 128)
        choice[16:32] = pltpu.roll(whole, 64, 1).reshape(16, 16, 128)
        place = (group * 2 + core) * depth_z + source

        def pick(leaf_to, cpl_to):
            row = cpl_to * depth_z + source
            return jnp.where(
                half,
                choice[take(row, 2 * leaf_to)],
                choice[take(row, 2 * leaf_to + 1)],
            )

        def send(r, carry):
            x_to, core_to, cpl_to = in_plane(r)
            leaf_to = leaf_at(x_to, z, core_to)
            outgoing[r, source] = pick(leaf_to, cpl_to)
            pltpu.make_async_remote_copy(
                src_ref=outgoing.at[r, source],
                dst_ref=incoming.at[place, pl.ds(quarter, 16)],
                send_sem=a2a_send.at[r],
                recv_sem=a2a_recv.at[(group * 2 + core) * SHARE + col],
                device_id=(leaf_to, cpl_to),
                device_id_type=MESH,
            ).start()
            return carry

        lax.fori_loop(1, plane, send, 0, unroll=4)
        incoming[place, pl.ds(quarter, 16)] = pick(me, col)

    def ring_step(k):
        sources = (lax.rem(z + depth_z - k, depth_z), lax.rem(z + k, depth_z))
        for way in range(2):
            if k <= hops[way]:
                everything = pl.ds(0, 16)
                here = shares.at[sources[way], everything]
                ring_copy(k - 1, way, everything, sources[way], here).wait()
                if k < hops[way]:
                    ring_copy(k, way, everything, sources[way], here).start()
        for way in range(2):
            if k <= hops[way]:
                give(sources[way])

    target = target_ref[...]
    slot = slot_ref[...]
    member = (target == row_of((32, BLK))).astype(f32)
    before = (row_of((BLK, BLK)) < lane_of((BLK, BLK))).astype(bf16)
    earlier = nn(member.astype(bf16), before)
    count = jnp.sum(member, axis=1, keepdims=True).astype(i32)
    even = ((count + 1) // 2) * 2
    even = jnp.where(row_of((32, 1)) < BOX, even, 0)
    below = (lane_of((32, 32)) < row_of((32, 32))).astype(bf16)
    start = nn(below, jnp.broadcast_to(even.astype(f32), (32, 128)).astype(bf16))
    start_v[...] = (start * 0.5).astype(i32)
    base = jnp.where(row_of((32, 1)) < BOX, start[:, :1], 4.0 * POS)
    rank = jnp.sum(member * (earlier + base), axis=0, keepdims=True).astype(i32)
    chosen = rank == row_of((POS, BLK))
    chosen_b = chosen.astype(bf16)
    pair_of = slot // 2
    pair_of = (
        (pair_of // GROUP) * GROUP
        + lax.rem(pair_of, 2) * depth_z
        + lax.rem(pair_of, GROUP) // 2
    )
    pair_row = jnp.broadcast_to(pair_of.astype(f32), (16, BLK)).astype(bf16)
    index_v[...] = nt(pair_row, chosen_b)[:8].astype(i32)
    odd = (slot - (slot // 2) * 2).astype(f32)
    odd_col = jnp.sum(jnp.where(chosen, odd, 0.0), axis=1, keepdims=True)
    half_f = (lane_of((POS, 128)) >= 64).astype(f32)
    used_half = (half_f == odd_col).astype(f32)
    copies = [
        pltpu.make_async_copy(index_v, index_s, local_sem.at[7]),
        pltpu.make_async_copy(start_v, start_s, local_sem.at[8]),
    ]
    for copy in copies:
        copy.start()

    plan_done.wait()
    give(z)

    def unpack(tile):
        return jnp.concatenate([tile[:, :64], tile[:, 64:]], axis=0)

    def pack(value):
        return jnp.concatenate([value[:8], value[8:]], axis=1)

    loads[5].wait()
    loads[6].wait()
    for step in range(1, GROUP):
        top_copy(step, mate(step)).wait()
    depth = GROUP.bit_length() - 1
    for k in range(GROUP // 2):
        group_coef[GROUP // 2 + k] = unpack(top_in[2 * k] + top_in[2 * k + 1])
    for level in range(depth - 2, -1, -1):
        for k in range(1 << level):
            child = 2 * ((1 << level) + k)
            children = jnp.concatenate([group_coef[child], group_coef[child + 1]], axis=1)
            matrix = ttr[pl.ds(((groups + group) << (level + 1)) + 2 * k - 2, 2)].reshape(128, 64)
            group_coef[(1 << level) + k] = wide(nn, children, matrix)
    group_out[...] = pack(group_coef[1])
    for step in range(1, groups):
        group_copy(step, group).start()
    group_in[group] = group_out[...]

    if hops[0] >= 1:
        ring_step(1)

    loads[4].wait()

    def turn(r, carry):
        x, y = cou[r], cou[r + 32]
        d = nt(chosen_b, jnp.concatenate([x, x, y, y], axis=0))
        rows_f[pl.ds(r, POS, stride=64), :] = d[:, :128] * used_half
        rows_f[pl.ds(r + 32, POS, stride=64), :] = d[:, 128:] * used_half
        return carry

    lax.fori_loop(0, 16, turn, 0, unroll=4)
    if hops[0] >= 2:
        ring_step(2)
    lax.fori_loop(16, 32, turn, 0, unroll=4)

    for step in range(1, groups):
        group_copy(step, lax.rem(group + step, groups)).wait()
    for k in range(groups):
        upper_coef[groups + k] = unpack(group_in[k])
    for k in range(groups - 1, 1, -1):
        children = jnp.concatenate([upper_coef[2 * k], upper_coef[2 * k + 1]], axis=1)
        upper_coef[k] = wide(nn, children, ttr[2 * k - 2 : 2 * k].reshape(128, 64))
    down = None
    for level in range(1, height):
        node = (n_leaf + me) // (1 << (height - level))
        sibling = node + 1 - 2 * lax.rem(node, 2)
        below = level - (groups.bit_length() - 1)
        if below <= 0:
            beside = upper_coef[sibling]
        else:
            beside = group_coef[sibling - ((groups + group) << below) + (1 << below)]
        here = wide(nt, beside, tco[node - 2])
        down = here if down is None else here + wide(nt, down, ttr[node - 2])
    top_share[...] = pack(down)

    def down_copy(step, source):
        return pltpu.make_async_remote_copy(
            src_ref=top_share,
            dst_ref=top_all.at[source],
            send_sem=down_send.at[step],
            recv_sem=down_recv.at[source],
            device_id=(me, other(step)),
            device_id_type=MESH,
        )

    for step in range(1, SHARE):
        down_copy(step, col).start()
    top_all[col] = top_share[...]

    if hops[0] >= 3:
        ring_step(3)

    def narrow(j, carry):
        blocks[j] = rows_f[pl.ds(pl.multiple_of(j * 64, 64), 64), :].astype(bf16)
        return carry

    lax.fori_loop(0, POS, narrow, 0, unroll=8)
    if hops[0] >= 4:
        ring_step(4)
    for copy in copies:
        copy.wait()

    loads[3].wait()
    for halo in halos:
        halo.wait()
    window = pl.ds(pl.multiple_of(col * 256, 256), 512)
    emb_t = emb[:, window]
    vec_t = vec[:, window]
    emb_w = emb_t.T
    squares = emb_w.astype(f32) * emb_w.astype(f32)
    norm_w = jnp.sum(squares, axis=1, keepdims=True)
    for a in range(2):
        own = emb_t[:, 128 * (a + 1) : 128 * (a + 2)]
        own_f = own.astype(f32)
        own_norm = jnp.sum(own_f * own_f, axis=0, keepdims=True)
        lo = 128 * a + 64
        inner = nn(emb_w[lo : lo + 256], own)
        distance = jnp.sqrt(jnp.maximum(norm_w[lo : lo + 256] + own_norm - 2.0 * inner, 0.0))
        scaled = sqrt_three * distance
        value = (1.0 + scaled) * jnp.exp(-scaled)
        row, lane = row_of((256, 128)), lane_of((256, 128))
        gap = row // 64 - lane // 64
        live = (gap >= 0) & (gap <= 2)
        if a == 0:
            live = live & ((row >= 64) | (me + col > 0))
        else:
            live = live & ((row < 192) | (me * SHARE + col < n_leaf * SHARE - 1))
        value = jnp.where(live, value, 0.0).astype(bf16)
        blank = jnp.zeros((64, 128), bf16)
        value = jnp.concatenate([blank, value, blank], axis=0)
        near_ref[:, 128 * a : 128 * (a + 1)] = nn(vec_t[:, 128 * a : 128 * a + 384], value)

    for step in range(1, SHARE):
        down_copy(step, other(step)).wait()
    parent = jnp.concatenate([unpack(top_all[q]) for q in range(SHARE)], axis=0)
    parent = wide(nt, parent, tra[0])
    parent = wide(nt, parent, tra[1 + col // 2])
    parent = wide(nt, parent, tra[3 + col])
    parent = wide(nt, parent, tra[pl.ds(7 + 2 * col, 2)].reshape(128, 64))
    from_top = []
    for a in range(2):
        w = tra[pl.ds(15 + 4 * col + 2 * a, 2)].reshape(128, 64)
        from_top.append(wide(nt, parent[:, 64 * a : 64 * (a + 1)], w))

    def arrived(r, carry):
        x_at, core_at, cpl_at = in_plane(r)
        from_core = x_at * 2 + core_at
        pltpu.make_async_remote_copy(
            src_ref=outgoing.at[r],
            dst_ref=incoming.at[
                pl.ds(pl.multiple_of(from_core * depth_z, depth_z), depth_z),
                pl.ds(pl.multiple_of(cpl_at * 16, 16), 16),
            ],
            send_sem=a2a_send.at[r],
            recv_sem=a2a_recv.at[from_core * SHARE + cpl_at],
            device_id=(leaf_at(x_at, z, core_at), cpl_at),
            device_id_type=MESH,
        ).wait()
        return carry

    lax.fori_loop(1, plane, arrived, 0)

    prefix[0] = jnp.zeros((64, 64), f32)

    def from_pair(j):
        return jnp.clip(index_s[0, j], 0, n_leaf - 1)

    def couple(u, acc):
        source = jnp.concatenate(
            [incoming[from_pair(2 * u)], incoming[from_pair(2 * u + 1)]], axis=1
        )
        matrix = jnp.concatenate([blocks[2 * u], blocks[2 * u + 1]], axis=1)
        acc = acc + nt(source, matrix)
        prefix[u + 1] = acc
        return acc

    lax.fori_loop(0, STEPS, couple, jnp.zeros((64, 64), f32), unroll=48)

    def run(m):
        return jnp.clip(start_s[m, 0], 0, STEPS)

    def field(m):
        return prefix[run(m + 1)] - prefix[run(m)]

    def pair(a, b):
        return jnp.concatenate([field(a), field(b)], axis=1)

    line = pair(1, 2) + wide(nt, field(0), tra[1:3].reshape(128, 64))
    lines = [line]
    for level in range(2, 5):
        first = (1 << level) - 1
        lower = []
        for j, tile in enumerate(lines):
            both = wide(nt, tile, lifts[len(lines) - 1 + j])
            lower.append(pair(first + 4 * j, first + 4 * j + 1) + both[:, :128])
            lower.append(pair(first + 4 * j + 2, first + 4 * j + 3) + both[:, 128:])
        lines = lower
    for j, tile in enumerate(lines):
        leaf_f[j] = tile
        leaf_b[j] = tile.astype(bf16)

    def field_copy(step, source):
        return pltpu.make_async_remote_copy(
            src_ref=leaf_b.at[pl.ds(2 * other(step), 2)],
            dst_ref=leaf_in.at[source],
            send_sem=field_send.at[step],
            recv_sem=field_recv.at[source],
            device_id=(me, other(step)),
            device_id_type=MESH,
        )

    for step in range(1, SHARE):
        field_copy(step, col).start()
    for step in range(1, SHARE):
        field_copy(step, other(step)).wait()

    for a in range(2):
        leaf = leaf_f[2 * col + a] + from_top[a]
        for step in range(1, SHARE):
            leaf = leaf + leaf_in[other(step), a].astype(f32)
        b = bas[:, pl.ds(pl.multiple_of(col * 256 + 128 * a, 128), 128)]
        out_ref[:, 128 * a : 128 * (a + 1)] = near_ref[:, 128 * a : 128 * (a + 1)] + nn(
            leaf.astype(bf16), spread(b)
        )


def body(
    vectors, embeddings, basis, transfer, coupling, top_transfer, top_coupling,
    send_boxes, block_slot, block_target,
):
    n_leaf = lax.axis_size("leaf")
    tops = top_transfer.shape[0]
    plane = 2 * (n_leaf // GROUP) * SHARE
    hbm = pl.BlockSpec(memory_space=pl.ANY)
    vmem = pl.BlockSpec(memory_space=pltpu.VMEM)
    dma = pltpu.SemaphoreType.DMA
    result = pl.pallas_call(
        functools.partial(kernel, n_leaf),
        out_shape=jax.ShapeDtypeStruct((NRHS, SHARE * LEAF), f32),
        in_specs=[hbm] * 7 + [vmem] * 3,
        out_specs=vmem,
        scratch_shapes=[
            pltpu.VMEM((64, 1280), bf16),
            pltpu.VMEM((64, 1280), bf16),
            pltpu.VMEM((64, 1024), bf16),
            pltpu.VMEM((BOX, 64, 64), bf16),
            pltpu.VMEM((64, 64, BLK), bf16),
            pltpu.VMEM((tops, 64, 64), bf16),
            pltpu.VMEM((tops, 64, 64), bf16),
            pltpu.VMEM((16, 64, 128), bf16),
            pltpu.VMEM((GROUP // 2, 16, 16, 128), bf16),
            pltpu.VMEM((32, 16, 128), bf16),
            pltpu.VMEM((plane, GROUP // 2, 16, 128), bf16),
            pltpu.VMEM((n_leaf, 64, 128), bf16),
            pltpu.VMEM((64, 128), f32),
            pltpu.VMEM((1, 2 * n_leaf), i32),
            pltpu.VMEM((SHARE, GROUP // 2, 2 * n_leaf), i32),
            pltpu.VMEM((SHARE * GROUP // 2, 2 * n_leaf), i32),
            pltpu.SMEM((SHARE * GROUP // 2, 2 * n_leaf), i32),
            pltpu.VMEM((7, 256, 128), bf16),
            pltpu.VMEM((8, 128), f32),
            pltpu.VMEM((GROUP, 8, 128), f32),
            pltpu.VMEM((GROUP, 16, 64), f32),
            pltpu.VMEM((8, 128), f32),
            pltpu.VMEM((n_leaf // GROUP, 8, 128), f32),
            pltpu.VMEM((2 * n_leaf // GROUP, 16, 64), f32),
            pltpu.VMEM((8, 128), f32),
            pltpu.VMEM((SHARE, 8, 128), f32),
            pltpu.VMEM((8, POS), i32),
            pltpu.VMEM((32, 128), i32),
            pltpu.SMEM((8, POS), i32),
            pltpu.SMEM((32, 128), i32),
            pltpu.VMEM((POS * 64 + 64, 128), f32),
            pltpu.VMEM((POS, 64, 128), bf16),
            pltpu.VMEM((STEPS + 1, 64, 64), f32),
            pltpu.VMEM((B_DEV // 2, 64, 128), f32),
            pltpu.VMEM((B_DEV // 2, 64, 128), bf16),
            pltpu.VMEM((SHARE, 2, 64, 128), bf16),
            pltpu.VMEM((64, SHARE * LEAF), f32),
            dma((10,)),
            dma((4,)),
            dma((4,)),
            dma((SHARE * GROUP // 2,)),
            dma((SHARE * GROUP // 2,)),
            dma((2, GROUP // 2)),
            dma((GROUP // 2,)),
            dma((plane,)),
            dma((plane,)),
            dma((GROUP,)),
            dma((GROUP,)),
            dma((n_leaf // GROUP,)),
            dma((n_leaf // GROUP,)),
            dma((SHARE,)),
            dma((SHARE,)),
            dma((SHARE,)),
            dma((SHARE,)),
        ],
        compiler_params=pltpu.CompilerParams(
            collective_id=0, has_side_effects=True, vmem_limit_bytes=56 * 1024 * 1024
        ),
    )(
        vectors.T, embeddings.T, basis.T, transfer, jnp.transpose(coupling, (1, 2, 0)),
        top_transfer, top_coupling, send_boxes,
        block_slot.reshape(1, BLK), block_target.reshape(1, BLK),
    )
    return result.T


def solution(mesh):
    placed = (
        P("leaf", None),
        P("leaf", None),
        P("leaf", None),
        P("leaf", None, None),
        P(("leaf", "cpl"), None, None),
        P(),
        P(),
        P("leaf", "cpl", None),
        P(("leaf", "cpl")),
        P(("leaf", "cpl")),
    )
    return jax.shard_map(
        body, mesh=mesh, in_specs=placed, out_specs=P(("leaf", "cpl"), None), check_vma=False
    )
```

```python
import functools

import jax
import jax.numpy as jnp
from jax import lax
from jax.experimental import pallas as pl
from jax.experimental.pallas import tpu as pltpu
from jax.sharding import PartitionSpec as P

RANK = 64
NRHS = 64
LEAF = 64
B_DEV = 16
BOX = 2 * B_DEV - 1
BLK = 256
SHARE = 4
POS = 288
STEPS = POS // 2
GROUP = 16

MESH = pl.DeviceIdType.MESH
f32, bf16, i32 = jnp.float32, jnp.bfloat16, jnp.int32
sqrt_three = 1.7320508075688772


def nn(a, b):
    return lax.dot_general(a, b, (((1,), (0,)), ((), ())), preferred_element_type=f32)


def nt(a, b):
    return lax.dot_general(a, b, (((1,), (1,)), ((), ())), preferred_element_type=f32)


def split_rows(x):
    upper = x.astype(bf16)
    lower = (x - upper.astype(f32)).astype(bf16)
    return jnp.concatenate([upper, lower], axis=0)


def wide(dot, x, w):
    rows = x.shape[0]
    y = dot(split_rows(x), w)
    return y[:rows] + y[rows:]


def lane_of(shape):
    return lax.broadcasted_iota(i32, shape, 1)


def row_of(shape):
    return lax.broadcasted_iota(i32, shape, 0)


def spread(tile):
    left = lane_of(tile.shape) < 64
    none = jnp.zeros_like(tile)
    return jnp.concatenate([jnp.where(left, tile, none), jnp.where(left, none, tile)], axis=0)


def kernel(
    n_leaf,
    vec_h, emb_h, bas_h, tra_h, cou_h, ttr_h, tco_h, plan_h, slot_h, target_h,
    out_ref,
    vec, emb, bas, tra, cou, ttr, tco,
    tiles_out, shares, choice, outgoing, incoming, root_dup, slot_ref, target_ref, plan_own, plan_in, plan_v, plan_s,
    lifts, top_out, top_in, group_coef, group_out, group_in, upper_coef, top_share, top_all,
    index_v, start_v, index_s, start_s,
    rows_f, blocks, prefix, leaf_f, leaf_b, leaf_in, near_ref,
    local_sem, halo_send, halo_recv, plan_send, plan_recv, ring_send, ring_recv,
    a2a_send, a2a_recv, top_send, top_recv,
    group_send, group_recv, field_send, field_recv, down_send, down_recv,
):
    height = n_leaf.bit_length() - 1
    me = lax.axis_index("leaf")
    col = lax.axis_index("cpl")

    group = me // GROUP
    groups = n_leaf // GROUP
    inside = lax.rem(me, GROUP)
    depth_z = GROUP // 2
    plane = 2 * groups * SHARE
    z = inside // 2
    core = lax.rem(inside, 2)

    def leaf_at(x, z_at, c):
        return x * GROUP + z_at * 2 + c

    def other(step):
        return lax.rem(col + step, SHARE)

    def mate(step):
        return lax.rem(inside + step, GROUP)

    def in_plane(r):
        return (
            lax.rem(group + r // (2 * SHARE), groups),
            lax.rem(core + lax.rem(r // SHARE, 2), 2),
            other(lax.rem(r, SHARE)),
        )

    def in_column(r):
        return lax.rem(z + r // SHARE, depth_z), other(lax.rem(r, SHARE))

    next_leaf = lax.rem(me + 1, n_leaf)
    last_leaf = lax.rem(me + n_leaf - 1, n_leaf)

    loads = [
        pltpu.make_async_copy(vec_h, vec.at[:, pl.ds(128, 1024)], local_sem.at[0]),
        pltpu.make_async_copy(bas_h, bas, local_sem.at[1]),
        pltpu.make_async_copy(tra_h, tra, local_sem.at[2]),
        pltpu.make_async_copy(emb_h, emb.at[:, pl.ds(128, 1024)], local_sem.at[3]),
        pltpu.make_async_copy(cou_h, cou, local_sem.at[4]),
        pltpu.make_async_copy(ttr_h, ttr, local_sem.at[5]),
        pltpu.make_async_copy(tco_h, tco, local_sem.at[6]),
    ]
    small = [
        pltpu.make_async_copy(plan_h.at[0], plan_own, local_sem.at[10]),
        pltpu.make_async_copy(slot_h, slot_ref, local_sem.at[11]),
        pltpu.make_async_copy(target_h, target_ref, local_sem.at[12]),
    ]
    for load in loads[:3] + small:
        load.start()

    barrier = pltpu.get_barrier_semaphore()

    def greet(leaf, cpl):
        pl.semaphore_signal(barrier, inc=1, device_id=(leaf, cpl), device_id_type=MESH)

    def greet_plane(r, carry):
        x_at, core_at, cpl_at = in_plane(r)
        greet(leaf_at(x_at, z, core_at), cpl_at)
        return carry

    def greet_column(r, carry):
        z_at, cpl_at = in_column(r)
        greet(leaf_at(group, z_at, core), cpl_at)
        return carry

    def greet_mate(step, carry):
        greet(group * GROUP + mate(step), col)
        return carry

    lax.fori_loop(1, plane, greet_plane, 0, unroll=True)
    lax.fori_loop(SHARE, depth_z * SHARE, greet_column, 0, unroll=True)
    lax.fori_loop(1, GROUP, greet_mate, 0, unroll=True)
    greet(next_leaf, col)
    greet(last_leaf, col)
    greetings = plane - 1 + (depth_z - 1) * SHARE + GROUP - 1 + 2

    loads[0].wait()
    loads[1].wait()
    tiles = []
    for j in range(B_DEV // 2):
        v = vec[:, 128 * (j + 1) : 128 * (j + 2)]
        tiles.append(nt(v, spread(bas[:, 128 * j : 128 * (j + 1)])))

    def keep_pair(first, tile):
        tiles_out[(first + 1) // 2] = tile.astype(bf16)

    first = B_DEV - 1
    for j, tile in enumerate(tiles):
        keep_pair(first + 2 * j, tile)
    loads[2].wait()
    for load in loads[3:]:
        load.start()

    while len(tiles) > 1:
        raised = []
        for j in range(len(tiles) // 2):
            w = tra[first + 4 * j : first + 4 * j + 4].reshape(256, 64)
            w = jnp.concatenate([w, w], axis=1)
            w = jnp.where((row_of(w.shape) < 128) == (lane_of(w.shape) < 64), w, jnp.zeros_like(w))
            lifts[len(tiles) // 2 - 1 + j] = w
            raised.append(wide(nn, jnp.concatenate(tiles[2 * j : 2 * j + 2], axis=1), w))
        first = (first - 1) // 2
        tiles = raised
        for j, tile in enumerate(tiles):
            keep_pair(first + 2 * j, tile)
    w = tra[1:3].reshape(128, 64)
    root = wide(nn, tiles[0], jnp.concatenate([w, w], axis=1))
    tiles_out[0] = root.astype(bf16)
    pl.semaphore_wait(barrier, greetings)

    quarter = pl.multiple_of(col * 16, 16)

    def ring_copy(hop, way, tiles_at, source, src):
        return pltpu.make_async_remote_copy(
            src_ref=src,
            dst_ref=shares.at[source, tiles_at],
            send_sem=ring_send.at[way, hop],
            recv_sem=ring_recv.at[source],
            device_id=(leaf_at(group, lax.rem(z + (1, depth_z - 1)[way], depth_z), core), col),
            device_id_type=MESH,
        )

    hops = (depth_z // 2, depth_z // 2 - 1)

    def ring_own(tiles_at):
        for way in range(2):
            if hops[way] > 0:
                ring_copy(
                    0, way, tiles_at, z, tiles_out.at[tiles_at, pl.ds(quarter, 16)]
                ).start()

    ring_own(pl.ds(0, 16))
    shares[z] = tiles_out[:, pl.ds(quarter, 16)]

    small[0].wait()

    def plan_copy(r, z_at, cpl_at):
        z_to, cpl_to = in_column(r)
        return pltpu.make_async_remote_copy(
            src_ref=plan_own,
            dst_ref=plan_in.at[cpl_at, pl.ds(z_at, 1)],
            send_sem=plan_send.at[r],
            recv_sem=plan_recv.at[cpl_at * depth_z + z_at],
            device_id=(leaf_at(group, z_to, core), cpl_to),
            device_id_type=MESH,
        )

    def give_plan(r, carry):
        plan_copy(r, z, col).start()
        return carry

    lax.fori_loop(1, depth_z * SHARE, give_plan, 0, unroll=True)
    plan_in[col, pl.ds(z, 1)] = plan_own[...]

    w = tra[0]
    root_dup[...] = wide(nn, root[:, :64], jnp.concatenate([w, w], axis=1))
    half8 = lane_of((8, 128)) < 64
    top_out[...] = jnp.where(
        half8, root_dup[pl.ds(quarter, 8), :], root_dup[pl.ds(pl.multiple_of(quarter + 8, 8), 8), :]
    )

    def top_copy(step, source):
        return pltpu.make_async_remote_copy(
            src_ref=top_out,
            dst_ref=top_in.at[source],
            send_sem=top_send.at[step],
            recv_sem=top_recv.at[source],
            device_id=(group * GROUP + mate(step), col),
            device_id_type=MESH,
        )

    def group_copy(step, source):
        return pltpu.make_async_remote_copy(
            src_ref=group_out,
            dst_ref=group_in.at[source],
            send_sem=group_send.at[step],
            recv_sem=group_recv.at[source],
            device_id=(lax.rem(group + step, groups) * GROUP + inside, col),
            device_id_type=MESH,
        )

    for step in range(1, GROUP):
        top_copy(step, inside).start()
    top_in[inside] = top_out[...]

    halos = []
    for k, (src_h, dst) in enumerate(((vec_h, vec), (emb_h, emb))):
        for side, (lanes, to, at) in enumerate(
            ((pl.ds(896, 128), next_leaf, 0), (pl.ds(0, 128), last_leaf, 1152))
        ):
            halos.append(
                pltpu.make_async_remote_copy(
                    src_ref=src_h.at[:, lanes],
                    dst_ref=dst.at[:, pl.ds(at, 128)],
                    send_sem=halo_send.at[2 * k + side],
                    recv_sem=halo_recv.at[2 * k + side],
                    device_id=(to, col),
                    device_id_type=MESH,
                )
            )
            halos[-1].start()

    def plan_wait(r, carry):
        z_at, cpl_at = in_column(r)
        plan_copy(r, z_at, cpl_at).wait()
        return carry

    half = lane_of((16, 128)) < 64

    def take(row, lane):
        return plan_s[row, lane]

    def give(source):
        whole = shares[source].reshape(256, 128)
        choice[0:16] = whole.reshape(16, 16, 128)
        choice[16:32] = pltpu.roll(whole, 64, 1).reshape(16, 16, 128)
        place = (group * 2 + core) * depth_z + source

        def pick(leaf_to, cpl_to):
            row = cpl_to * depth_z + source
            return jnp.where(
                half,
                choice[take(row, 2 * leaf_to)],
                choice[take(row, 2 * leaf_to + 1)],
            )

        def send(r, carry):
            x_to, core_to, cpl_to = in_plane(r)
            leaf_to = leaf_at(x_to, z, core_to)
            outgoing[r, source] = pick(leaf_to, cpl_to)
            pltpu.make_async_remote_copy(
                src_ref=outgoing.at[r, source],
                dst_ref=incoming.at[place, pl.ds(quarter, 16)],
                send_sem=a2a_send.at[r],
                recv_sem=a2a_recv.at[(group * 2 + core) * SHARE + col],
                device_id=(leaf_to, cpl_to),
                device_id_type=MESH,
            ).start()
            return carry

        lax.fori_loop(1, plane, send, 0, unroll=31)
        incoming[place, pl.ds(quarter, 16)] = pick(me, col)

    def ring_step(k):
        sources = (lax.rem(z + depth_z - k, depth_z), lax.rem(z + k, depth_z))
        for way in range(2):
            if k <= hops[way]:
                everything = pl.ds(0, 16)
                here = shares.at[sources[way], everything]
                ring_copy(k - 1, way, everything, sources[way], here).wait()
                if k < hops[way]:
                    ring_copy(k, way, everything, sources[way], here).start()
        for way in range(2):
            if k <= hops[way]:
                give(sources[way])

    lax.fori_loop(1, depth_z * SHARE, plan_wait, 0)
    box = plan_in[...].reshape(SHARE * depth_z, 2 * n_leaf)
    even_box = box - (box // 2) * 2 == 0
    even_slot = lax.rem(lane_of(box.shape), 2) == 0
    plan_v[...] = (box + 1) // 2 + jnp.where(even_box == even_slot, 16, 0)
    plan_done = pltpu.make_async_copy(plan_v, plan_s, local_sem.at[9])
    plan_done.start()
    small[1].wait()
    small[2].wait()
    target = target_ref[...]
    slot = slot_ref[...]
    member = (target == row_of((32, BLK))).astype(f32)
    before = (row_of((BLK, BLK)) < lane_of((BLK, BLK))).astype(bf16)
    earlier = nn(member.astype(bf16), before)
    count = jnp.sum(member, axis=1, keepdims=True).astype(i32)
    even = ((count + 1) // 2) * 2
    even = jnp.where(row_of((32, 1)) < BOX, even, 0)
    below = (lane_of((32, 32)) < row_of((32, 32))).astype(bf16)
    start = nn(below, jnp.broadcast_to(even.astype(f32), (32, 128)).astype(bf16))
    start_v[...] = (start * 0.5).astype(i32)
    base = jnp.where(row_of((32, 1)) < BOX, start[:, :1], 4.0 * POS)
    rank = jnp.sum(member * (earlier + base), axis=0, keepdims=True).astype(i32)
    chosen = rank == row_of((POS, BLK))
    chosen_b = chosen.astype(bf16)
    pair_of = slot // 2
    pair_of = (
        (pair_of // GROUP) * GROUP
        + lax.rem(pair_of, 2) * depth_z
        + lax.rem(pair_of, GROUP) // 2
    )
    pair_row = jnp.broadcast_to(pair_of.astype(f32), (16, BLK)).astype(bf16)
    index_v[...] = nt(pair_row, chosen_b)[:8].astype(i32)
    odd = (slot - (slot // 2) * 2).astype(f32)
    odd_col = jnp.sum(jnp.where(chosen, odd, 0.0), axis=1, keepdims=True)
    half_f = (lane_of((POS, 128)) >= 64).astype(f32)
    used_half = (half_f == odd_col).astype(f32)
    copies = [
        pltpu.make_async_copy(index_v, index_s, local_sem.at[7]),
        pltpu.make_async_copy(start_v, start_s, local_sem.at[8]),
    ]
    for copy in copies:
        copy.start()

    plan_done.wait()
    give(z)

    if hops[0] >= 1:
        ring_step(1)

    def unpack(tile):
        return jnp.concatenate([tile[:, :64], tile[:, 64:]], axis=0)

    def pack(value):
        return jnp.concatenate([value[:8], value[8:]], axis=1)

    loads[5].wait()
    loads[6].wait()
    for step in range(1, GROUP):
        top_copy(step, mate(step)).wait()
    depth = GROUP.bit_length() - 1
    for k in range(GROUP // 2):
        group_coef[GROUP // 2 + k] = unpack(top_in[2 * k] + top_in[2 * k + 1])
    for level in range(depth - 2, -1, -1):
        for k in range(1 << level):
            child = 2 * ((1 << level) + k)
            children = jnp.concatenate([group_coef[child], group_coef[child + 1]], axis=1)
            matrix = ttr[pl.ds(((groups + group) << (level + 1)) + 2 * k - 2, 2)].reshape(128, 64)
            group_coef[(1 << level) + k] = wide(nn, children, matrix)
    group_out[...] = pack(group_coef[1])
    for step in range(1, groups):
        group_copy(step, group).start()
    group_in[group] = group_out[...]

    if hops[0] >= 2:
        ring_step(2)

    loads[4].wait()

    def turn(r, carry):
        x, y = cou[r], cou[r + 32]
        d = nt(chosen_b, jnp.concatenate([x, x, y, y], axis=0))
        rows_f[pl.ds(r, POS, stride=65), :] = d[:, :128] * used_half
        rows_f[pl.ds(r + 32, POS, stride=65), :] = d[:, 128:] * used_half
        return carry

    lax.fori_loop(0, 16, turn, 0, unroll=4)

    if hops[0] >= 3:
        ring_step(3)

    lax.fori_loop(16, 32, turn, 0, unroll=4)

    if hops[0] >= 4:
        ring_step(4)

    for step in range(1, groups):
        group_copy(step, lax.rem(group + step, groups)).wait()
    for k in range(groups):
        upper_coef[groups + k] = unpack(group_in[k])
    for k in range(groups - 1, 1, -1):
        children = jnp.concatenate([upper_coef[2 * k], upper_coef[2 * k + 1]], axis=1)
        upper_coef[k] = wide(nn, children, ttr[2 * k - 2 : 2 * k].reshape(128, 64))
    down = None
    for level in range(1, height):
        node = (n_leaf + me) // (1 << (height - level))
        sibling = node + 1 - 2 * lax.rem(node, 2)
        below = level - (groups.bit_length() - 1)
        if below <= 0:
            beside = upper_coef[sibling]
        else:
            beside = group_coef[sibling - ((groups + group) << below) + (1 << below)]
        here = wide(nt, beside, tco[node - 2])
        down = here if down is None else here + wide(nt, down, ttr[node - 2])
    top_share[...] = pack(down)

    def down_copy(step, source):
        return pltpu.make_async_remote_copy(
            src_ref=top_share,
            dst_ref=top_all.at[source],
            send_sem=down_send.at[step],
            recv_sem=down_recv.at[source],
            device_id=(me, other(step)),
            device_id_type=MESH,
        )

    for step in range(1, SHARE):
        down_copy(step, col).start()
    top_all[col] = top_share[...]

    def narrow(j, carry):
        blocks[j] = rows_f[pl.ds(j * 65, 64), :].astype(bf16)
        return carry

    lax.fori_loop(0, POS, narrow, 0, unroll=8)
    loads[3].wait()
    for halo in halos:
        halo.wait()
    window = pl.ds(pl.multiple_of(col * 256, 256), 512)
    emb_t = emb[:, window]
    vec_t = vec[:, window]
    emb_w = emb_t.T
    squares = emb_w.astype(f32) * emb_w.astype(f32)
    norm_w = jnp.sum(squares, axis=1, keepdims=True)
    for a in range(2):
        own = emb_t[:, 128 * (a + 1) : 128 * (a + 2)]
        own_f = own.astype(f32)
        own_norm = jnp.sum(own_f * own_f, axis=0, keepdims=True)
        lo = 128 * a + 64
        inner = nn(emb_w[lo : lo + 256], own)
        distance = jnp.sqrt(jnp.maximum(norm_w[lo : lo + 256] + own_norm - 2.0 * inner, 0.0))
        scaled = sqrt_three * distance
        value = (1.0 + scaled) * jnp.exp(-scaled)
        row, lane = row_of((256, 128)), lane_of((256, 128))
        gap = row // 64 - lane // 64
        live = (gap >= 0) & (gap <= 2)
        if a == 0:
            live = live & ((row >= 64) | (me + col > 0))
        else:
            live = live & ((row < 192) | (me * SHARE + col < n_leaf * SHARE - 1))
        value = jnp.where(live, value, 0.0).astype(bf16)
        blank = jnp.zeros((64, 128), bf16)
        value = jnp.concatenate([blank, value, blank], axis=0)
        near_ref[:, 128 * a : 128 * (a + 1)] = nn(vec_t[:, 128 * a : 128 * a + 384], value)

    for step in range(1, SHARE):
        down_copy(step, other(step)).wait()
    parent = jnp.concatenate([unpack(top_all[q]) for q in range(SHARE)], axis=0)
    parent = wide(nt, parent, tra[0])
    parent = wide(nt, parent, tra[1 + col // 2])
    parent = wide(nt, parent, tra[3 + col])
    parent = wide(nt, parent, tra[pl.ds(7 + 2 * col, 2)].reshape(128, 64))
    from_top = []
    for a in range(2):
        w = tra[pl.ds(15 + 4 * col + 2 * a, 2)].reshape(128, 64)
        from_top.append(wide(nt, parent[:, 64 * a : 64 * (a + 1)], w))

    for copy in copies:
        copy.wait()


    def arrived(r, carry):
        x_at, core_at, cpl_at = in_plane(r)
        from_core = x_at * 2 + core_at
        pltpu.make_async_remote_copy(
            src_ref=outgoing.at[r],
            dst_ref=incoming.at[
                pl.ds(pl.multiple_of(from_core * depth_z, depth_z), depth_z),
                pl.ds(pl.multiple_of(cpl_at * 16, 16), 16),
            ],
            send_sem=a2a_send.at[r],
            recv_sem=a2a_recv.at[from_core * SHARE + cpl_at],
            device_id=(leaf_at(x_at, z, core_at), cpl_at),
            device_id_type=MESH,
        ).wait()
        return carry

    lax.fori_loop(1, plane, arrived, 0)

    prefix[0] = jnp.zeros((64, 64), f32)

    def from_pair(j):
        return jnp.clip(index_s[0, j], 0, n_leaf - 1)

    def couple(u, acc):
        source = jnp.concatenate(
            [incoming[from_pair(2 * u)], incoming[from_pair(2 * u + 1)]], axis=1
        )
        matrix = jnp.concatenate([blocks[2 * u], blocks[2 * u + 1]], axis=1)
        acc = acc + nt(source, matrix)
        prefix[u + 1] = acc
        return acc

    lax.fori_loop(0, STEPS, couple, jnp.zeros((64, 64), f32), unroll=48)

    def run(m):
        return jnp.clip(start_s[m, 0], 0, STEPS)

    def field(m):
        return prefix[run(m + 1)] - prefix[run(m)]

    def pair(a, b):
        return jnp.concatenate([field(a), field(b)], axis=1)

    line = pair(1, 2) + wide(nt, field(0), tra[1:3].reshape(128, 64))
    lines = [line]
    for level in range(2, 5):
        first = (1 << level) - 1
        lower = []
        for j, tile in enumerate(lines):
            both = wide(nt, tile, lifts[len(lines) - 1 + j])
            lower.append(pair(first + 4 * j, first + 4 * j + 1) + both[:, :128])
            lower.append(pair(first + 4 * j + 2, first + 4 * j + 3) + both[:, 128:])
        lines = lower
    for j, tile in enumerate(lines):
        leaf_f[j] = tile
        leaf_b[j] = tile.astype(bf16)

    def field_copy(step, source):
        return pltpu.make_async_remote_copy(
            src_ref=leaf_b.at[pl.ds(2 * other(step), 2)],
            dst_ref=leaf_in.at[source],
            send_sem=field_send.at[step],
            recv_sem=field_recv.at[source],
            device_id=(me, other(step)),
            device_id_type=MESH,
        )

    for step in range(1, SHARE):
        field_copy(step, col).start()
    for step in range(1, SHARE):
        field_copy(step, other(step)).wait()

    for a in range(2):
        leaf = leaf_f[2 * col + a] + from_top[a]
        for step in range(1, SHARE):
            leaf = leaf + leaf_in[other(step), a].astype(f32)
        b = bas[:, pl.ds(pl.multiple_of(col * 256 + 128 * a, 128), 128)]
        out_ref[:, 128 * a : 128 * (a + 1)] = near_ref[:, 128 * a : 128 * (a + 1)] + nn(
            leaf.astype(bf16), spread(b)
        )


def body(
    vectors, embeddings, basis, transfer, coupling, top_transfer, top_coupling,
    send_boxes, block_slot, block_target,
):
    n_leaf = lax.axis_size("leaf")
    tops = top_transfer.shape[0]
    plane = 2 * (n_leaf // GROUP) * SHARE
    hbm = pl.BlockSpec(memory_space=pl.ANY)
    vmem = pl.BlockSpec(memory_space=pltpu.VMEM)
    dma = pltpu.SemaphoreType.DMA
    result = pl.pallas_call(
        functools.partial(kernel, n_leaf),
        out_shape=jax.ShapeDtypeStruct((NRHS, SHARE * LEAF), f32),
        in_specs=[hbm] * 10,
        out_specs=vmem,
        scratch_shapes=[
            pltpu.VMEM((64, 1280), bf16),
            pltpu.VMEM((64, 1280), bf16),
            pltpu.VMEM((64, 1024), bf16),
            pltpu.VMEM((BOX, 64, 64), bf16),
            pltpu.VMEM((64, 64, BLK), bf16),
            pltpu.VMEM((tops, 64, 64), bf16),
            pltpu.VMEM((tops, 64, 64), bf16),
            pltpu.VMEM((16, 64, 128), bf16),
            pltpu.VMEM((GROUP // 2, 16, 16, 128), bf16),
            pltpu.VMEM((32, 16, 128), bf16),
            pltpu.VMEM((plane, GROUP // 2, 16, 128), bf16),
            pltpu.VMEM((n_leaf, 64, 128), bf16),
            pltpu.VMEM((64, 128), f32),
            pltpu.VMEM((1, BLK), i32),
            pltpu.VMEM((1, BLK), i32),
            pltpu.VMEM((1, 2 * n_leaf), i32),
            pltpu.VMEM((SHARE, GROUP // 2, 2 * n_leaf), i32),
            pltpu.VMEM((SHARE * GROUP // 2, 2 * n_leaf), i32),
            pltpu.SMEM((SHARE * GROUP // 2, 2 * n_leaf), i32),
            pltpu.VMEM((7, 256, 128), bf16),
            pltpu.VMEM((8, 128), f32),
            pltpu.VMEM((GROUP, 8, 128), f32),
            pltpu.VMEM((GROUP, 16, 64), f32),
            pltpu.VMEM((8, 128), f32),
            pltpu.VMEM((n_leaf // GROUP, 8, 128), f32),
            pltpu.VMEM((2 * n_leaf // GROUP, 16, 64), f32),
            pltpu.VMEM((8, 128), f32),
            pltpu.VMEM((SHARE, 8, 128), f32),
            pltpu.VMEM((8, POS), i32),
            pltpu.VMEM((32, 128), i32),
            pltpu.SMEM((8, POS), i32),
            pltpu.SMEM((32, 128), i32),
            pltpu.VMEM((POS * 65 + 65, 128), f32),
            pltpu.VMEM((POS, 64, 128), bf16),
            pltpu.VMEM((STEPS + 1, 64, 64), f32),
            pltpu.VMEM((B_DEV // 2, 64, 128), f32),
            pltpu.VMEM((B_DEV // 2, 64, 128), bf16),
            pltpu.VMEM((SHARE, 2, 64, 128), bf16),
            pltpu.VMEM((64, SHARE * LEAF), f32),
            dma((13,)),
            dma((4,)),
            dma((4,)),
            dma((SHARE * GROUP // 2,)),
            dma((SHARE * GROUP // 2,)),
            dma((2, GROUP // 2)),
            dma((GROUP // 2,)),
            dma((plane,)),
            dma((plane,)),
            dma((GROUP,)),
            dma((GROUP,)),
            dma((n_leaf // GROUP,)),
            dma((n_leaf // GROUP,)),
            dma((SHARE,)),
            dma((SHARE,)),
            dma((SHARE,)),
            dma((SHARE,)),
        ],
        compiler_params=pltpu.CompilerParams(
            collective_id=0, has_side_effects=True, vmem_limit_bytes=56 * 1024 * 1024
        ),
    )(
        vectors.T, embeddings.T, basis.T, transfer, jnp.transpose(coupling, (1, 2, 0)),
        top_transfer, top_coupling, send_boxes,
        block_slot.reshape(1, BLK), block_target.reshape(1, BLK),
    )
    return result.T


def solution(mesh):
    placed = (
        P("leaf", None),
        P("leaf", None),
        P("leaf", None),
        P("leaf", None, None),
        P(("leaf", "cpl"), None, None),
        P(),
        P(),
        P("leaf", "cpl", None),
        P(("leaf", "cpl")),
        P(("leaf", "cpl")),
    )
    return jax.shard_map(
        body, mesh=mesh, in_specs=placed, out_specs=P(("leaf", "cpl"), None), check_vma=False
    )
```

```python
import functools

import jax
import jax.numpy as jnp
from jax import lax
from jax.experimental import pallas as pl
from jax.experimental.pallas import tpu as pltpu
from jax.sharding import PartitionSpec as P

RANK = 64
NRHS = 64
LEAF = 64
B_DEV = 16
BOX = 2 * B_DEV - 1
BLK = 256
SHARE = 4
POS = 288
STEPS = POS // 2
GROUP = 16
DEPTH = 8
NEAR_Z = (0, -1, 1, -2, 2, -3, 3)

MESH = pl.DeviceIdType.MESH
f32, bf16, i32 = jnp.float32, jnp.bfloat16, jnp.int32
sqrt_three = 1.7320508075688772


def nn(a, b):
    return lax.dot_general(a, b, (((1,), (0,)), ((), ())), preferred_element_type=f32)


def nt(a, b):
    return lax.dot_general(a, b, (((1,), (1,)), ((), ())), preferred_element_type=f32)


def split_rows(x):
    upper = x.astype(bf16)
    lower = (x - upper.astype(f32)).astype(bf16)
    return jnp.concatenate([upper, lower], axis=0)


def wide(dot, x, w):
    rows = x.shape[0]
    y = dot(split_rows(x), w)
    return y[:rows] + y[rows:]


def lane_of(shape):
    return lax.broadcasted_iota(i32, shape, 1)


def row_of(shape):
    return lax.broadcasted_iota(i32, shape, 0)


def spread(tile):
    left = lane_of(tile.shape) < 64
    none = jnp.zeros_like(tile)
    return jnp.concatenate([jnp.where(left, tile, none), jnp.where(left, none, tile)], axis=0)


def kernel(
    n_leaf,
    vec_h, emb_h, bas_h, tra_h, cou_h, ttr_h, tco_h, plan_h, slot_h, target_h,
    out_ref,
    vec, emb, bas, tra, cou, ttr, tco,
    tiles_out, shares, choice, outgoing, incoming, root_dup, slot_ref, target_ref, plan_own, plan_in, plan_v, plan_s,
    lifts, top_out, top_in, group_coef, group_out, group_in, upper_coef, top_share, top_all,
    index_v, start_v, index_s, start_s,
    rows_f, blocks, prefix, leaf_f, leaf_b, leaf_in, near_ref,
    local_sem, halo_send, halo_recv, plan_send, plan_recv, ring_send, ring_recv,
    a2a_send, a2a_recv, top_send, top_recv,
    group_send, group_recv, field_send, field_recv, down_send, down_recv,
):
    height = n_leaf.bit_length() - 1
    me = lax.axis_index("leaf")
    col = lax.axis_index("cpl")

    group = me // GROUP
    groups = n_leaf // GROUP
    inside = lax.rem(me, GROUP)
    depth_z = DEPTH
    plane = 2 * groups * SHARE
    z = inside // 2
    core = lax.rem(inside, 2)

    def leaf_at(x, z_at, c):
        return x * GROUP + z_at * 2 + c

    def other(step):
        return lax.rem(col + step, SHARE)

    def mate(step):
        return lax.rem(inside + step, GROUP)

    def in_plane(r):
        return (
            lax.rem(group + r // (2 * SHARE), groups),
            lax.rem(core + lax.rem(r // SHARE, 2), 2),
            other(lax.rem(r, SHARE)),
        )

    def z_by(step):
        return lax.rem(z + step + depth_z, depth_z)

    far = 2 * core - 1

    next_leaf = lax.rem(me + 1, n_leaf)
    last_leaf = lax.rem(me + n_leaf - 1, n_leaf)

    loads = [
        pltpu.make_async_copy(vec_h, vec.at[:, pl.ds(128, 1024)], local_sem.at[0]),
        pltpu.make_async_copy(bas_h, bas, local_sem.at[1]),
        pltpu.make_async_copy(tra_h, tra, local_sem.at[2]),
        pltpu.make_async_copy(emb_h, emb.at[:, pl.ds(128, 1024)], local_sem.at[3]),
        pltpu.make_async_copy(cou_h, cou, local_sem.at[4]),
        pltpu.make_async_copy(ttr_h, ttr, local_sem.at[5]),
        pltpu.make_async_copy(tco_h, tco, local_sem.at[6]),
    ]
    small = [
        pltpu.make_async_copy(plan_h.at[0], plan_own, local_sem.at[10]),
        pltpu.make_async_copy(slot_h, slot_ref, local_sem.at[11]),
        pltpu.make_async_copy(target_h, target_ref, local_sem.at[12]),
    ]
    for load in loads[:3] + small:
        load.start()

    plan_in[...] = jnp.zeros_like(plan_in)

    barrier = pltpu.get_barrier_semaphore()

    def greet(leaf, cpl):
        pl.semaphore_signal(barrier, inc=1, device_id=(leaf, cpl), device_id_type=MESH)

    def greet_plane(r, carry):
        x_at, core_at, cpl_at = in_plane(r)
        greet(leaf_at(x_at, z, core_at), cpl_at)
        return carry

    def greet_beside(r, carry):
        x_at, core_at, cpl_at = in_plane(r)
        greet(leaf_at(x_at, z_by(1 - 2 * core_at), core_at), cpl_at)
        return carry

    lax.fori_loop(1, plane, greet_plane, 0, unroll=True)
    lax.fori_loop(0, plane, greet_beside, 0, unroll=True)
    for step in range(SHARE):
        for hop in NEAR_Z[1:]:
            greet(leaf_at(group, z_by(hop), core), other(step))
    for step in range(1, GROUP):
        greet(group * GROUP + mate(step), col)
    greet(next_leaf, col)
    greet(last_leaf, col)
    greetings = 2 * plane - 1 + (len(NEAR_Z) - 1) * SHARE + GROUP - 1 + 2

    loads[0].wait()
    loads[1].wait()
    tiles = []
    for j in range(B_DEV // 2):
        v = vec[:, 128 * (j + 1) : 128 * (j + 2)]
        tiles.append(nt(v, spread(bas[:, 128 * j : 128 * (j + 1)])))

    def keep_pair(first, tile):
        tiles_out[(first + 1) // 2] = tile.astype(bf16)

    first = B_DEV - 1
    for j, tile in enumerate(tiles):
        keep_pair(first + 2 * j, tile)
    loads[2].wait()
    for load in loads[3:]:
        load.start()

    while len(tiles) > 1:
        raised = []
        for j in range(len(tiles) // 2):
            w = tra[first + 4 * j : first + 4 * j + 4].reshape(256, 64)
            w = jnp.concatenate([w, w], axis=1)
            w = jnp.where((row_of(w.shape) < 128) == (lane_of(w.shape) < 64), w, jnp.zeros_like(w))
            lifts[len(tiles) // 2 - 1 + j] = w
            raised.append(wide(nn, jnp.concatenate(tiles[2 * j : 2 * j + 2], axis=1), w))
        first = (first - 1) // 2
        tiles = raised
        for j, tile in enumerate(tiles):
            keep_pair(first + 2 * j, tile)
    w = tra[1:3].reshape(128, 64)
    root = wide(nn, tiles[0], jnp.concatenate([w, w], axis=1))
    tiles_out[0] = root.astype(bf16)
    pl.semaphore_wait(barrier, greetings)

    quarter = pl.multiple_of(col * 16, 16)

    def ring_copy(place, src):
        way = lax.rem(place + 1, 2)
        return pltpu.make_async_remote_copy(
            src_ref=src,
            dst_ref=shares.at[place],
            send_sem=ring_send.at[place],
            recv_sem=ring_recv.at[place],
            device_id=(leaf_at(group, z_by(1 - 2 * way), core), col),
            device_id_type=MESH,
        )

    own_share = tiles_out.at[:, pl.ds(quarter, 16)]
    for place in (1, 2):
        ring_copy(place, own_share).start()
    shares[0] = tiles_out[:, pl.ds(quarter, 16)]

    small[0].wait()

    def plan_copy(place, step, cpl_at):
        return pltpu.make_async_remote_copy(
            src_ref=plan_own,
            dst_ref=plan_in.at[cpl_at, pl.ds(place, 1)],
            send_sem=plan_send.at[place * SHARE + step],
            recv_sem=plan_recv.at[cpl_at * DEPTH + place],
            device_id=(leaf_at(group, z_by(-NEAR_Z[place]), core), other(step)),
            device_id_type=MESH,
        )

    plan_pairs = [(p, step) for p in range(len(NEAR_Z)) for step in range(SHARE) if p + step > 0]
    for place, step in plan_pairs:
        plan_copy(place, step, col).start()
    plan_in[col, 0:1] = plan_own[...]

    w = tra[0]
    root_dup[...] = wide(nn, root[:, :64], jnp.concatenate([w, w], axis=1))
    half8 = lane_of((8, 128)) < 64
    top_out[...] = jnp.where(
        half8, root_dup[pl.ds(quarter, 8), :], root_dup[pl.ds(pl.multiple_of(quarter + 8, 8), 8), :]
    )

    def top_copy(step, source):
        return pltpu.make_async_remote_copy(
            src_ref=top_out,
            dst_ref=top_in.at[source],
            send_sem=top_send.at[step],
            recv_sem=top_recv.at[source],
            device_id=(group * GROUP + mate(step), col),
            device_id_type=MESH,
        )

    def group_copy(step, source):
        return pltpu.make_async_remote_copy(
            src_ref=group_out,
            dst_ref=group_in.at[source],
            send_sem=group_send.at[step],
            recv_sem=group_recv.at[source],
            device_id=(lax.rem(group + step, groups) * GROUP + inside, col),
            device_id_type=MESH,
        )

    for step in range(1, GROUP):
        top_copy(step, inside).start()
    top_in[inside] = top_out[...]

    halos = []
    for k, (src_h, dst) in enumerate(((vec_h, vec), (emb_h, emb))):
        for side, (lanes, to, at) in enumerate(
            ((pl.ds(896, 128), next_leaf, 0), (pl.ds(0, 128), last_leaf, 1152))
        ):
            halos.append(
                pltpu.make_async_remote_copy(
                    src_ref=src_h.at[:, lanes],
                    dst_ref=dst.at[:, pl.ds(at, 128)],
                    send_sem=halo_send.at[2 * k + side],
                    recv_sem=halo_recv.at[2 * k + side],
                    device_id=(to, col),
                    device_id_type=MESH,
                )
            )
            halos[-1].start()

    half = lane_of((16, 128)) < 64

    def take(row, lane):
        return plan_s[row, lane]

    def ready(place):
        whole = shares[place].reshape(256, 128)
        choice[0:16] = whole.reshape(16, 16, 128)
        choice[16:32] = pltpu.roll(whole, 64, 1).reshape(16, 16, 128)

    def give(place, kind):
        slot_at = place if kind == 0 else DEPTH - 1
        to_z = z_by(far * kind)
        from_core = group * 2 + core

        def pick(leaf_to, cpl_to):
            row = cpl_to * DEPTH + place
            return jnp.where(
                half, choice[take(row, 2 * leaf_to)], choice[take(row, 2 * leaf_to + 1)]
            )

        def send(r, carry):
            x_to, core_to, cpl_to = in_plane(r)
            leaf_to = leaf_at(x_to, to_z, core_to)
            outgoing[r, slot_at] = pick(leaf_to, cpl_to)
            pltpu.make_async_remote_copy(
                src_ref=outgoing.at[r, slot_at],
                dst_ref=incoming.at[from_core * DEPTH + slot_at, pl.ds(quarter, 16)],
                send_sem=a2a_send.at[kind, r],
                recv_sem=a2a_recv.at[kind, from_core * SHARE + col],
                device_id=(leaf_to, cpl_to),
                device_id_type=MESH,
            ).start()
            return carry

        lax.fori_loop(1 if kind == 0 else 0, plane, send, 0, unroll=True)
        if kind == 0:
            incoming[from_core * DEPTH + slot_at, pl.ds(quarter, 16)] = pick(me, col)

    small[1].wait()
    small[2].wait()
    target = target_ref[...]
    slot = slot_ref[...]
    member = (target == row_of((32, BLK))).astype(f32)
    before = (row_of((BLK, BLK)) < lane_of((BLK, BLK))).astype(bf16)
    earlier = nn(member.astype(bf16), before)
    count = jnp.sum(member, axis=1, keepdims=True).astype(i32)
    even = ((count + 1) // 2) * 2
    even = jnp.where(row_of((32, 1)) < BOX, even, 0)
    below = (lane_of((32, 32)) < row_of((32, 32))).astype(bf16)
    start = nn(below, jnp.broadcast_to(even.astype(f32), (32, 128)).astype(bf16))
    start_v[...] = (start * 0.5).astype(i32)
    base = jnp.where(row_of((32, 1)) < BOX, start[:, :1], 4.0 * POS)
    rank = jnp.sum(member * (earlier + base), axis=0, keepdims=True).astype(i32)
    chosen = rank == row_of((POS, BLK))
    chosen_b = chosen.astype(bf16)
    pair_of = slot // 2
    apart = lax.rem(lax.rem(pair_of, GROUP) // 2 - z + depth_z, depth_z)
    place_of = jnp.where(apart < depth_z // 2, 2 * apart, 2 * (depth_z - apart) - 1)
    pair_of = (
        (pair_of // GROUP) * GROUP
        + lax.rem(pair_of, 2) * depth_z
        + place_of
    )
    pair_row = jnp.broadcast_to(pair_of.astype(f32), (16, BLK)).astype(bf16)
    index_v[...] = nt(pair_row, chosen_b)[:8].astype(i32)
    odd = (slot - (slot // 2) * 2).astype(f32)
    odd_col = jnp.sum(jnp.where(chosen, odd, 0.0), axis=1, keepdims=True)
    half_f = (lane_of((POS, 128)) >= 64).astype(f32)
    used_half = (half_f == odd_col).astype(f32)
    copies = [
        pltpu.make_async_copy(index_v, index_s, local_sem.at[7]),
        pltpu.make_async_copy(start_v, start_s, local_sem.at[8]),
    ]
    for copy in copies:
        copy.start()

    for place, step in plan_pairs:
        plan_copy(place, step, other(step)).wait()
    box = plan_in[...].reshape(SHARE * depth_z, 2 * n_leaf)
    even_box = box - (box // 2) * 2 == 0
    even_slot = lax.rem(lane_of(box.shape), 2) == 0
    plan_v[...] = (box + 1) // 2 + jnp.where(even_box == even_slot, 16, 0)
    plan_done = pltpu.make_async_copy(plan_v, plan_s, local_sem.at[9])
    plan_done.start()
    for place in (1, 2):
        ring_copy(place, own_share).wait()
        ring_copy(place + 2, shares.at[place]).start()
    plan_done.wait()
    ready(0)
    give(0, 0)

    for place in (1, 2):
        ready(place)
        give(place, 0)

    def unpack(tile):
        return jnp.concatenate([tile[:, :64], tile[:, 64:]], axis=0)

    def pack(value):
        return jnp.concatenate([value[:8], value[8:]], axis=1)

    loads[5].wait()
    loads[6].wait()
    for step in range(1, GROUP):
        top_copy(step, mate(step)).wait()
    depth = GROUP.bit_length() - 1
    for k in range(GROUP // 2):
        group_coef[GROUP // 2 + k] = unpack(top_in[2 * k] + top_in[2 * k + 1])
    for level in range(depth - 2, -1, -1):
        for k in range(1 << level):
            child = 2 * ((1 << level) + k)
            children = jnp.concatenate([group_coef[child], group_coef[child + 1]], axis=1)
            matrix = ttr[pl.ds(((groups + group) << (level + 1)) + 2 * k - 2, 2)].reshape(128, 64)
            group_coef[(1 << level) + k] = wide(nn, children, matrix)
    group_out[...] = pack(group_coef[1])
    for step in range(1, groups):
        group_copy(step, group).start()
    group_in[group] = group_out[...]

    for place in (3, 4):
        ring_copy(place, shares.at[place - 2]).wait()
        ring_copy(place + 2, shares.at[place]).start()
    for place in (3, 4):
        ready(place)
        give(place, 0)

    loads[4].wait()

    def turn(r, carry):
        x, y = cou[r], cou[r + 32]
        d = nt(chosen_b, jnp.concatenate([x, x, y, y], axis=0))
        rows_f[pl.ds(r, POS, stride=65), :] = d[:, :128] * used_half
        rows_f[pl.ds(r + 32, POS, stride=65), :] = d[:, 128:] * used_half
        return carry

    lax.fori_loop(0, 16, turn, 0, unroll=8)

    for place in (5, 6):
        ring_copy(place, shares.at[place - 2]).wait()
    ready(6 - core)
    give(6 - core, 1)
    for place in (5, 6):
        ready(place)
        give(place, 0)

    lax.fori_loop(16, 32, turn, 0, unroll=8)

    for step in range(1, groups):
        group_copy(step, lax.rem(group + step, groups)).wait()
    for k in range(groups):
        upper_coef[groups + k] = unpack(group_in[k])
    for k in range(groups - 1, 1, -1):
        children = jnp.concatenate([upper_coef[2 * k], upper_coef[2 * k + 1]], axis=1)
        upper_coef[k] = wide(nn, children, ttr[2 * k - 2 : 2 * k].reshape(128, 64))
    down = None
    for level in range(1, height):
        node = (n_leaf + me) // (1 << (height - level))
        sibling = node + 1 - 2 * lax.rem(node, 2)
        below = level - (groups.bit_length() - 1)
        if below <= 0:
            beside = upper_coef[sibling]
        else:
            beside = group_coef[sibling - ((groups + group) << below) + (1 << below)]
        here = wide(nt, beside, tco[node - 2])
        down = here if down is None else here + wide(nt, down, ttr[node - 2])
    top_share[...] = pack(down)

    def down_copy(step, source):
        return pltpu.make_async_remote_copy(
            src_ref=top_share,
            dst_ref=top_all.at[source],
            send_sem=down_send.at[step],
            recv_sem=down_recv.at[source],
            device_id=(me, other(step)),
            device_id_type=MESH,
        )

    for step in range(1, SHARE):
        down_copy(step, col).start()
    top_all[col] = top_share[...]

    def narrow(j, carry):
        blocks[j] = rows_f[pl.ds(j * 65, 64), :].astype(bf16)
        return carry

    lax.fori_loop(0, POS, narrow, 0, unroll=8)
    loads[3].wait()
    for halo in halos:
        halo.wait()
    window = pl.ds(pl.multiple_of(col * 256, 256), 512)
    emb_t = emb[:, window]
    vec_t = vec[:, window]
    emb_w = emb_t.T
    squares = emb_w.astype(f32) * emb_w.astype(f32)
    norm_w = jnp.sum(squares, axis=1, keepdims=True)
    for a in range(2):
        own = emb_t[:, 128 * (a + 1) : 128 * (a + 2)]
        own_f = own.astype(f32)
        own_norm = jnp.sum(own_f * own_f, axis=0, keepdims=True)
        lo = 128 * a + 64
        inner = nn(emb_w[lo : lo + 256], own)
        distance = jnp.sqrt(jnp.maximum(norm_w[lo : lo + 256] + own_norm - 2.0 * inner, 0.0))
        scaled = sqrt_three * distance
        value = (1.0 + scaled) * jnp.exp(-scaled)
        row, lane = row_of((256, 128)), lane_of((256, 128))
        gap = row // 64 - lane // 64
        live = (gap >= 0) & (gap <= 2)
        if a == 0:
            live = live & ((row >= 64) | (me + col > 0))
        else:
            live = live & ((row < 192) | (me * SHARE + col < n_leaf * SHARE - 1))
        value = jnp.where(live, value, 0.0).astype(bf16)
        blank = jnp.zeros((64, 128), bf16)
        value = jnp.concatenate([blank, value, blank], axis=0)
        near_ref[:, 128 * a : 128 * (a + 1)] = nn(vec_t[:, 128 * a : 128 * a + 384], value)

    for step in range(1, SHARE):
        down_copy(step, other(step)).wait()
    parent = jnp.concatenate([unpack(top_all[q]) for q in range(SHARE)], axis=0)
    parent = wide(nt, parent, tra[0])
    parent = wide(nt, parent, tra[1 + col // 2])
    parent = wide(nt, parent, tra[3 + col])
    parent = wide(nt, parent, tra[pl.ds(7 + 2 * col, 2)].reshape(128, 64))
    from_top = []
    for a in range(2):
        w = tra[pl.ds(15 + 4 * col + 2 * a, 2)].reshape(128, 64)
        from_top.append(wide(nt, parent[:, 64 * a : 64 * (a + 1)], w))

    for copy in copies:
        copy.wait()


    def arrived(kind):
        def wait(r, carry):
            x_at, core_at, cpl_at = in_plane(r)
            from_core = x_at * 2 + core_at
            many = DEPTH - 1 if kind == 0 else 1
            slots = pl.ds(kind * (DEPTH - 1), many)
            first = from_core * DEPTH + kind * (DEPTH - 1)
            pltpu.make_async_remote_copy(
                src_ref=outgoing.at[r, slots],
                dst_ref=incoming.at[
                    pl.ds(first, many),
                    pl.ds(pl.multiple_of(cpl_at * 16, 16), 16),
                ],
                send_sem=a2a_send.at[kind, r],
                recv_sem=a2a_recv.at[kind, from_core * SHARE + cpl_at],
                device_id=(leaf_at(x_at, z_by(far * kind), core_at), cpl_at),
                device_id_type=MESH,
            ).wait()
            return carry

        lax.fori_loop(1 if kind == 0 else 0, plane, wait, 0)

    for kind in range(2):
        arrived(kind)

    prefix[0] = jnp.zeros((64, 64), f32)

    def from_pair(j):
        return jnp.clip(index_s[0, j], 0, n_leaf - 1)

    def couple(u, acc):
        source = jnp.concatenate(
            [incoming[from_pair(2 * u)], incoming[from_pair(2 * u + 1)]], axis=1
        )
        matrix = jnp.concatenate([blocks[2 * u], blocks[2 * u + 1]], axis=1)
        acc = acc + nt(source, matrix)
        prefix[u + 1] = acc
        return acc

    lax.fori_loop(0, STEPS, couple, jnp.zeros((64, 64), f32), unroll=True)

    def run(m):
        return jnp.clip(start_s[m, 0], 0, STEPS)

    def field(m):
        return prefix[run(m + 1)] - prefix[run(m)]

    def pair(a, b):
        return jnp.concatenate([field(a), field(b)], axis=1)

    line = pair(1, 2) + wide(nt, field(0), tra[1:3].reshape(128, 64))
    lines = [line]
    for level in range(2, 5):
        first = (1 << level) - 1
        lower = []
        for j, tile in enumerate(lines):
            both = wide(nt, tile, lifts[len(lines) - 1 + j])
            lower.append(pair(first + 4 * j, first + 4 * j + 1) + both[:, :128])
            lower.append(pair(first + 4 * j + 2, first + 4 * j + 3) + both[:, 128:])
        lines = lower
    for j, tile in enumerate(lines):
        leaf_f[j] = tile
        leaf_b[j] = tile.astype(bf16)

    def field_copy(step, source):
        return pltpu.make_async_remote_copy(
            src_ref=leaf_b.at[pl.ds(2 * other(step), 2)],
            dst_ref=leaf_in.at[source],
            send_sem=field_send.at[step],
            recv_sem=field_recv.at[source],
            device_id=(me, other(step)),
            device_id_type=MESH,
        )

    for step in range(1, SHARE):
        field_copy(step, col).start()
    for step in range(1, SHARE):
        field_copy(step, other(step)).wait()

    for a in range(2):
        leaf = leaf_f[2 * col + a] + from_top[a]
        for step in range(1, SHARE):
            leaf = leaf + leaf_in[other(step), a].astype(f32)
        b = bas[:, pl.ds(pl.multiple_of(col * 256 + 128 * a, 128), 128)]
        out_ref[:, 128 * a : 128 * (a + 1)] = near_ref[:, 128 * a : 128 * (a + 1)] + nn(
            leaf.astype(bf16), spread(b)
        )


def body(
    vectors, embeddings, basis, transfer, coupling, top_transfer, top_coupling,
    send_boxes, block_slot, block_target,
):
    n_leaf = lax.axis_size("leaf")
    tops = top_transfer.shape[0]
    plane = 2 * (n_leaf // GROUP) * SHARE
    hbm = pl.BlockSpec(memory_space=pl.ANY)
    vmem = pl.BlockSpec(memory_space=pltpu.VMEM)
    dma = pltpu.SemaphoreType.DMA
    result = pl.pallas_call(
        functools.partial(kernel, n_leaf),
        out_shape=jax.ShapeDtypeStruct((NRHS, SHARE * LEAF), f32),
        in_specs=[hbm] * 10,
        out_specs=vmem,
        scratch_shapes=[
            pltpu.VMEM((64, 1280), bf16),
            pltpu.VMEM((64, 1280), bf16),
            pltpu.VMEM((64, 1024), bf16),
            pltpu.VMEM((BOX, 64, 64), bf16),
            pltpu.VMEM((64, 64, BLK), bf16),
            pltpu.VMEM((tops, 64, 64), bf16),
            pltpu.VMEM((tops, 64, 64), bf16),
            pltpu.VMEM((16, 64, 128), bf16),
            pltpu.VMEM((7, 16, 16, 128), bf16),
            pltpu.VMEM((32, 16, 128), bf16),
            pltpu.VMEM((plane, GROUP // 2, 16, 128), bf16),
            pltpu.VMEM((n_leaf, 64, 128), bf16),
            pltpu.VMEM((64, 128), f32),
            pltpu.VMEM((1, BLK), i32),
            pltpu.VMEM((1, BLK), i32),
            pltpu.VMEM((1, 2 * n_leaf), i32),
            pltpu.VMEM((SHARE, GROUP // 2, 2 * n_leaf), i32),
            pltpu.VMEM((SHARE * GROUP // 2, 2 * n_leaf), i32),
            pltpu.SMEM((SHARE * GROUP // 2, 2 * n_leaf), i32),
            pltpu.VMEM((7, 256, 128), bf16),
            pltpu.VMEM((8, 128), f32),
            pltpu.VMEM((GROUP, 8, 128), f32),
            pltpu.VMEM((GROUP, 16, 64), f32),
            pltpu.VMEM((8, 128), f32),
            pltpu.VMEM((n_leaf // GROUP, 8, 128), f32),
            pltpu.VMEM((2 * n_leaf // GROUP, 16, 64), f32),
            pltpu.VMEM((8, 128), f32),
            pltpu.VMEM((SHARE, 8, 128), f32),
            pltpu.VMEM((8, POS), i32),
            pltpu.VMEM((32, 128), i32),
            pltpu.SMEM((8, POS), i32),
            pltpu.SMEM((32, 128), i32),
            pltpu.VMEM((POS * 65 + 65, 128), f32),
            pltpu.VMEM((POS, 64, 128), bf16),
            pltpu.VMEM((STEPS + 1, 64, 64), f32),
            pltpu.VMEM((B_DEV // 2, 64, 128), f32),
            pltpu.VMEM((B_DEV // 2, 64, 128), bf16),
            pltpu.VMEM((SHARE, 2, 64, 128), bf16),
            pltpu.VMEM((64, SHARE * LEAF), f32),
            dma((13,)),
            dma((4,)),
            dma((4,)),
            dma((7 * SHARE,)),
            dma((SHARE * DEPTH,)),
            dma((7,)),
            dma((7,)),
            dma((2, plane)),
            dma((2, plane)),
            dma((GROUP,)),
            dma((GROUP,)),
            dma((n_leaf // GROUP,)),
            dma((n_leaf // GROUP,)),
            dma((SHARE,)),
            dma((SHARE,)),
            dma((SHARE,)),
            dma((SHARE,)),
        ],
        compiler_params=pltpu.CompilerParams(
            collective_id=0, has_side_effects=True, vmem_limit_bytes=56 * 1024 * 1024
        ),
    )(
        vectors.T, embeddings.T, basis.T, transfer, jnp.transpose(coupling, (1, 2, 0)),
        top_transfer, top_coupling, send_boxes,
        block_slot.reshape(1, BLK), block_target.reshape(1, BLK),
    )
    return result.T


def solution(mesh):
    placed = (
        P("leaf", None),
        P("leaf", None),
        P("leaf", None),
        P("leaf", None, None),
        P(("leaf", "cpl"), None, None),
        P(),
        P(),
        P("leaf", "cpl", None),
        P(("leaf", "cpl")),
        P(("leaf", "cpl")),
    )
    return jax.shard_map(
        body, mesh=mesh, in_specs=placed, out_specs=P(("leaf", "cpl"), None), check_vma=False
    )
```

```python
import functools

import jax
import jax.numpy as jnp
from jax import lax
from jax.experimental import pallas as pl
from jax.experimental.pallas import tpu as pltpu
from jax.sharding import PartitionSpec as P

RANK = 64
NRHS = 64
LEAF = 64
B_DEV = 16
BOX = 2 * B_DEV - 1
BLK = 256
SHARE = 4
POS = 288
STEPS = POS // 2
GROUP = 16
DEPTH = 8
NEAR_Z = (0, -1, 1, -2, 2, -3, 3)

MESH = pl.DeviceIdType.MESH
f32, bf16, i32 = jnp.float32, jnp.bfloat16, jnp.int32
sqrt_three = 1.7320508075688772


def nn(a, b):
    return lax.dot_general(a, b, (((1,), (0,)), ((), ())), preferred_element_type=f32)


def nt(a, b):
    return lax.dot_general(a, b, (((1,), (1,)), ((), ())), preferred_element_type=f32)


def split_rows(x):
    upper = x.astype(bf16)
    lower = (x - upper.astype(f32)).astype(bf16)
    return jnp.concatenate([upper, lower], axis=0)


def wide(dot, x, w):
    rows = x.shape[0]
    y = dot(split_rows(x), w)
    return y[:rows] + y[rows:]


def lane_of(shape):
    return lax.broadcasted_iota(i32, shape, 1)


def row_of(shape):
    return lax.broadcasted_iota(i32, shape, 0)


def spread(tile):
    left = lane_of(tile.shape) < 64
    none = jnp.zeros_like(tile)
    return jnp.concatenate([jnp.where(left, tile, none), jnp.where(left, none, tile)], axis=0)


def kernel(
    n_leaf,
    vec_h, emb_h, bas_h, tra_h, cou_h, ttr_h, tco_h, plan_h, slot_h, target_h,
    out_ref,
    vec, emb, bas, tra, cou, ttr, tco,
    tiles_out, shares, choice, outgoing, incoming, root_dup, slot_ref, target_ref, plan_own, plan_in, plan_v, plan_s,
    lifts, top_out, top_in, group_coef, group_out, group_in, upper_coef, top_share, top_all,
    index_v, start_v, index_s, start_s,
    rows_f, blocks, prefix, leaf_f, leaf_b, leaf_in, near_ref,
    local_sem, halo_send, halo_recv, plan_send, plan_recv, ring_send, ring_recv,
    a2a_send, a2a_recv, top_send, top_recv,
    group_send, group_recv, field_send, field_recv, down_send, down_recv,
):
    height = n_leaf.bit_length() - 1
    me = lax.axis_index("leaf")
    col = lax.axis_index("cpl")

    group = me // GROUP
    groups = n_leaf // GROUP
    inside = lax.rem(me, GROUP)
    depth_z = DEPTH
    plane = 2 * groups * SHARE
    z = inside // 2
    core = lax.rem(inside, 2)

    def leaf_at(x, z_at, c):
        return x * GROUP + z_at * 2 + c

    def other(step):
        return lax.rem(col + step, SHARE)

    def mate(step):
        return lax.rem(inside + step, GROUP)

    def in_plane(r):
        return (
            lax.rem(group + r // (2 * SHARE), groups),
            lax.rem(core + lax.rem(r // SHARE, 2), 2),
            other(lax.rem(r, SHARE)),
        )

    def z_by(step):
        return lax.rem(z + step + depth_z, depth_z)

    far = 2 * core - 1

    next_leaf = lax.rem(me + 1, n_leaf)
    last_leaf = lax.rem(me + n_leaf - 1, n_leaf)

    loads = [
        pltpu.make_async_copy(vec_h, vec.at[:, pl.ds(128, 1024)], local_sem.at[0]),
        pltpu.make_async_copy(bas_h, bas, local_sem.at[1]),
        pltpu.make_async_copy(tra_h, tra, local_sem.at[2]),
        pltpu.make_async_copy(emb_h, emb.at[:, pl.ds(128, 1024)], local_sem.at[3]),
        pltpu.make_async_copy(cou_h, cou, local_sem.at[4]),
        pltpu.make_async_copy(ttr_h, ttr, local_sem.at[5]),
        pltpu.make_async_copy(tco_h, tco, local_sem.at[6]),
    ]
    small = [
        pltpu.make_async_copy(plan_h.at[0], plan_own, local_sem.at[10]),
        pltpu.make_async_copy(slot_h, slot_ref, local_sem.at[11]),
        pltpu.make_async_copy(target_h, target_ref, local_sem.at[12]),
    ]
    for load in loads[:3] + small:
        load.start()

    plan_in[...] = jnp.zeros_like(plan_in)

    barrier = pltpu.get_barrier_semaphore()

    def greet(leaf, cpl):
        pl.semaphore_signal(barrier, inc=1, device_id=(leaf, cpl), device_id_type=MESH)

    def greet_plane(r, carry):
        x_at, core_at, cpl_at = in_plane(r)
        greet(leaf_at(x_at, z, core_at), cpl_at)
        return carry

    def greet_beside(r, carry):
        x_at, core_at, cpl_at = in_plane(r)
        greet(leaf_at(x_at, z_by(1 - 2 * core_at), core_at), cpl_at)
        return carry

    lax.fori_loop(1, plane, greet_plane, 0, unroll=True)
    lax.fori_loop(0, plane, greet_beside, 0, unroll=True)
    for step in range(SHARE):
        for hop in NEAR_Z[1:]:
            greet(leaf_at(group, z_by(hop), core), other(step))
    for step in range(1, GROUP):
        greet(group * GROUP + mate(step), col)
    greet(next_leaf, col)
    greet(last_leaf, col)
    greetings = 2 * plane - 1 + (len(NEAR_Z) - 1) * SHARE + GROUP - 1 + 2

    loads[0].wait()
    loads[1].wait()
    tiles = []
    for j in range(B_DEV // 2):
        v = vec[:, 128 * (j + 1) : 128 * (j + 2)]
        tiles.append(nt(v, spread(bas[:, 128 * j : 128 * (j + 1)])))

    def keep_pair(first, tile):
        tiles_out[(first + 1) // 2] = tile.astype(bf16)

    first = B_DEV - 1
    for j, tile in enumerate(tiles):
        keep_pair(first + 2 * j, tile)
    loads[2].wait()
    for load in loads[3:]:
        load.start()

    while len(tiles) > 1:
        raised = []
        for j in range(len(tiles) // 2):
            w = tra[first + 4 * j : first + 4 * j + 4].reshape(256, 64)
            w = jnp.concatenate([w, w], axis=1)
            w = jnp.where((row_of(w.shape) < 128) == (lane_of(w.shape) < 64), w, jnp.zeros_like(w))
            lifts[len(tiles) // 2 - 1 + j] = w
            raised.append(wide(nn, jnp.concatenate(tiles[2 * j : 2 * j + 2], axis=1), w))
        first = (first - 1) // 2
        tiles = raised
        for j, tile in enumerate(tiles):
            keep_pair(first + 2 * j, tile)
    w = tra[1:3].reshape(128, 64)
    root = wide(nn, tiles[0], jnp.concatenate([w, w], axis=1))
    tiles_out[0] = root.astype(bf16)
    pl.semaphore_wait(barrier, greetings)

    quarter = pl.multiple_of(col * 16, 16)

    def ring_copy(place, src):
        way = lax.rem(place + 1, 2)
        return pltpu.make_async_remote_copy(
            src_ref=src,
            dst_ref=shares.at[place],
            send_sem=ring_send.at[place],
            recv_sem=ring_recv.at[place],
            device_id=(leaf_at(group, z_by(1 - 2 * way), core), col),
            device_id_type=MESH,
        )

    own_share = tiles_out.at[:, pl.ds(quarter, 16)]
    small[0].wait()

    def plan_copy(place, step, cpl_at):
        return pltpu.make_async_remote_copy(
            src_ref=plan_own,
            dst_ref=plan_in.at[cpl_at, pl.ds(place, 1)],
            send_sem=plan_send.at[place * SHARE + step],
            recv_sem=plan_recv.at[cpl_at * DEPTH + place],
            device_id=(leaf_at(group, z_by(-NEAR_Z[place]), core), other(step)),
            device_id_type=MESH,
        )

    plan_pairs = [(p, step) for p in range(len(NEAR_Z)) for step in range(SHARE) if p + step > 0]
    for place, step in plan_pairs:
        plan_copy(place, step, col).start()
    plan_in[col, 0:1] = plan_own[...]

    for place in (1, 2):
        ring_copy(place, own_share).start()
    shares[0] = tiles_out[:, pl.ds(quarter, 16)]

    w = tra[0]
    root_dup[...] = wide(nn, root[:, :64], jnp.concatenate([w, w], axis=1))
    half8 = lane_of((8, 128)) < 64
    top_out[...] = jnp.where(
        half8, root_dup[pl.ds(quarter, 8), :], root_dup[pl.ds(pl.multiple_of(quarter + 8, 8), 8), :]
    )

    def top_copy(step, source):
        return pltpu.make_async_remote_copy(
            src_ref=top_out,
            dst_ref=top_in.at[source],
            send_sem=top_send.at[step],
            recv_sem=top_recv.at[source],
            device_id=(group * GROUP + mate(step), col),
            device_id_type=MESH,
        )

    def group_copy(step, source):
        return pltpu.make_async_remote_copy(
            src_ref=group_out,
            dst_ref=group_in.at[source],
            send_sem=group_send.at[step],
            recv_sem=group_recv.at[source],
            device_id=(lax.rem(group + step, groups) * GROUP + inside, col),
            device_id_type=MESH,
        )

    for step in range(1, GROUP):
        top_copy(step, inside).start()
    top_in[inside] = top_out[...]

    halos = []
    for k, (src_h, dst) in enumerate(((vec_h, vec), (emb_h, emb))):
        for side, (lanes, to, at) in enumerate(
            ((pl.ds(896, 128), next_leaf, 0), (pl.ds(0, 128), last_leaf, 1152))
        ):
            halos.append(
                pltpu.make_async_remote_copy(
                    src_ref=src_h.at[:, lanes],
                    dst_ref=dst.at[:, pl.ds(at, 128)],
                    send_sem=halo_send.at[2 * k + side],
                    recv_sem=halo_recv.at[2 * k + side],
                    device_id=(to, col),
                    device_id_type=MESH,
                )
            )
            halos[-1].start()

    half = lane_of((16, 128)) < 64

    def take(row, lane):
        return plan_s[row, lane]

    def ready(place):
        whole = shares[place].reshape(256, 128)
        choice[0:16] = whole.reshape(16, 16, 128)
        choice[16:32] = pltpu.roll(whole, 64, 1).reshape(16, 16, 128)

    def give(place, kind):
        slot_at = place if kind == 0 else DEPTH - 1
        to_z = z_by(far * kind)
        from_core = group * 2 + core

        def pick(leaf_to, cpl_to):
            row = cpl_to * DEPTH + place
            return jnp.where(
                half, choice[take(row, 2 * leaf_to)], choice[take(row, 2 * leaf_to + 1)]
            )

        def send(r, carry):
            x_to, core_to, cpl_to = in_plane(r)
            leaf_to = leaf_at(x_to, to_z, core_to)
            outgoing[r, slot_at] = pick(leaf_to, cpl_to)
            pltpu.make_async_remote_copy(
                src_ref=outgoing.at[r, slot_at],
                dst_ref=incoming.at[from_core * DEPTH + slot_at, pl.ds(quarter, 16)],
                send_sem=a2a_send.at[kind, r],
                recv_sem=a2a_recv.at[kind, from_core * SHARE + col],
                device_id=(leaf_to, cpl_to),
                device_id_type=MESH,
            ).start()
            return carry

        lax.fori_loop(1 if kind == 0 else 0, plane, send, 0, unroll=True)
        if kind == 0:
            incoming[from_core * DEPTH + slot_at, pl.ds(quarter, 16)] = pick(me, col)

    small[1].wait()
    small[2].wait()
    target = target_ref[...]
    slot = slot_ref[...]
    member = (target == row_of((32, BLK))).astype(f32)
    before = (row_of((BLK, BLK)) < lane_of((BLK, BLK))).astype(bf16)
    earlier = nn(member.astype(bf16), before)
    count = jnp.sum(member, axis=1, keepdims=True).astype(i32)
    even = ((count + 1) // 2) * 2
    even = jnp.where(row_of((32, 1)) < BOX, even, 0)
    below = (lane_of((32, 32)) < row_of((32, 32))).astype(bf16)
    start = nn(below, jnp.broadcast_to(even.astype(f32), (32, 128)).astype(bf16))
    start_v[...] = (start * 0.5).astype(i32)
    base = jnp.where(row_of((32, 1)) < BOX, start[:, :1], 4.0 * POS)
    rank = jnp.sum(member * (earlier + base), axis=0, keepdims=True).astype(i32)
    chosen = rank == row_of((POS, BLK))
    chosen_b = chosen.astype(bf16)
    pair_of = slot // 2
    apart = lax.rem(lax.rem(pair_of, GROUP) // 2 - z + depth_z, depth_z)
    place_of = jnp.where(apart < depth_z // 2, 2 * apart, 2 * (depth_z - apart) - 1)
    pair_of = (
        (pair_of // GROUP) * GROUP
        + lax.rem(pair_of, 2) * depth_z
        + place_of
    )
    pair_row = jnp.broadcast_to(pair_of.astype(f32), (16, BLK)).astype(bf16)
    index_v[...] = nt(pair_row, chosen_b)[:8].astype(i32)
    odd = (slot - (slot // 2) * 2).astype(f32)
    odd_col = jnp.sum(jnp.where(chosen, odd, 0.0), axis=1, keepdims=True)
    half_f = (lane_of((POS, 128)) >= 64).astype(f32)
    used_half = (half_f == odd_col).astype(f32)
    copies = [
        pltpu.make_async_copy(index_v, index_s, local_sem.at[7]),
        pltpu.make_async_copy(start_v, start_s, local_sem.at[8]),
    ]
    for copy in copies:
        copy.start()

    for place, step in plan_pairs:
        plan_copy(place, step, other(step)).wait()
    box = plan_in[...].reshape(SHARE * depth_z, 2 * n_leaf)
    even_box = box - (box // 2) * 2 == 0
    even_slot = lax.rem(lane_of(box.shape), 2) == 0
    plan_v[...] = (box + 1) // 2 + jnp.where(even_box == even_slot, 16, 0)
    plan_done = pltpu.make_async_copy(plan_v, plan_s, local_sem.at[9])
    plan_done.start()
    for place in (1, 2):
        ring_copy(place, own_share).wait()
        ring_copy(place + 2, shares.at[place]).start()
    plan_done.wait()
    ready(0)
    give(0, 0)

    for place in (1, 2):
        ready(place)
        give(place, 0)

    def unpack(tile):
        return jnp.concatenate([tile[:, :64], tile[:, 64:]], axis=0)

    def pack(value):
        return jnp.concatenate([value[:8], value[8:]], axis=1)

    loads[5].wait()
    loads[6].wait()
    for step in range(1, GROUP):
        top_copy(step, mate(step)).wait()
    depth = GROUP.bit_length() - 1
    for k in range(GROUP // 2):
        group_coef[GROUP // 2 + k] = unpack(top_in[2 * k] + top_in[2 * k + 1])
    for level in range(depth - 2, -1, -1):
        for k in range(1 << level):
            child = 2 * ((1 << level) + k)
            children = jnp.concatenate([group_coef[child], group_coef[child + 1]], axis=1)
            matrix = ttr[pl.ds(((groups + group) << (level + 1)) + 2 * k - 2, 2)].reshape(128, 64)
            group_coef[(1 << level) + k] = wide(nn, children, matrix)
    group_out[...] = pack(group_coef[1])
    for step in range(1, groups):
        group_copy(step, group).start()
    group_in[group] = group_out[...]

    for place in (3, 4):
        ring_copy(place, shares.at[place - 2]).wait()
        ring_copy(place + 2, shares.at[place]).start()
    for place in (3, 4):
        ready(place)
        give(place, 0)

    loads[4].wait()

    def turn(r, carry):
        x, y = cou[r], cou[r + 32]
        d = nt(chosen_b, jnp.concatenate([x, x, y, y], axis=0))
        rows_f[pl.ds(r, POS, stride=65), :] = d[:, :128] * used_half
        rows_f[pl.ds(r + 32, POS, stride=65), :] = d[:, 128:] * used_half
        return carry

    lax.fori_loop(0, 16, turn, 0, unroll=8)

    for place in (5, 6):
        ring_copy(place, shares.at[place - 2]).wait()
    ready(6 - core)
    give(6 - core, 1)
    for place in (5, 6):
        ready(place)
        give(place, 0)

    lax.fori_loop(16, 32, turn, 0, unroll=8)

    for step in range(1, groups):
        group_copy(step, lax.rem(group + step, groups)).wait()
    for k in range(groups):
        upper_coef[groups + k] = unpack(group_in[k])
    for k in range(groups - 1, 1, -1):
        children = jnp.concatenate([upper_coef[2 * k], upper_coef[2 * k + 1]], axis=1)
        upper_coef[k] = wide(nn, children, ttr[2 * k - 2 : 2 * k].reshape(128, 64))
    down = None
    for level in range(1, height):
        node = (n_leaf + me) // (1 << (height - level))
        sibling = node + 1 - 2 * lax.rem(node, 2)
        below = level - (groups.bit_length() - 1)
        if below <= 0:
            beside = upper_coef[sibling]
        else:
            beside = group_coef[sibling - ((groups + group) << below) + (1 << below)]
        here = wide(nt, beside, tco[node - 2])
        down = here if down is None else here + wide(nt, down, ttr[node - 2])
    top_share[...] = pack(down)

    def down_copy(step, source):
        return pltpu.make_async_remote_copy(
            src_ref=top_share,
            dst_ref=top_all.at[source],
            send_sem=down_send.at[step],
            recv_sem=down_recv.at[source],
            device_id=(me, other(step)),
            device_id_type=MESH,
        )

    for step in range(1, SHARE):
        down_copy(step, col).start()
    top_all[col] = top_share[...]

    def narrow(j, carry):
        blocks[j] = rows_f[pl.ds(j * 65, 64), :].astype(bf16)
        return carry

    lax.fori_loop(0, POS, narrow, 0, unroll=8)
    loads[3].wait()
    for halo in halos:
        halo.wait()
    window = pl.ds(pl.multiple_of(col * 256, 256), 512)
    emb_t = emb[:, window]
    vec_t = vec[:, window]
    emb_w = emb_t.T
    squares = emb_w.astype(f32) * emb_w.astype(f32)
    norm_w = jnp.sum(squares, axis=1, keepdims=True)
    for a in range(2):
        own = emb_t[:, 128 * (a + 1) : 128 * (a + 2)]
        own_f = own.astype(f32)
        own_norm = jnp.sum(own_f * own_f, axis=0, keepdims=True)
        lo = 128 * a + 64
        inner = nn(emb_w[lo : lo + 256], own)
        distance = jnp.sqrt(jnp.maximum(norm_w[lo : lo + 256] + own_norm - 2.0 * inner, 0.0))
        scaled = sqrt_three * distance
        value = (1.0 + scaled) * jnp.exp(-scaled)
        row, lane = row_of((256, 128)), lane_of((256, 128))
        gap = row // 64 - lane // 64
        live = (gap >= 0) & (gap <= 2)
        if a == 0:
            live = live & ((row >= 64) | (me + col > 0))
        else:
            live = live & ((row < 192) | (me * SHARE + col < n_leaf * SHARE - 1))
        value = jnp.where(live, value, 0.0).astype(bf16)
        blank = jnp.zeros((64, 128), bf16)
        value = jnp.concatenate([blank, value, blank], axis=0)
        near_ref[:, 128 * a : 128 * (a + 1)] = nn(vec_t[:, 128 * a : 128 * a + 384], value)

    for step in range(1, SHARE):
        down_copy(step, other(step)).wait()
    parent = jnp.concatenate([unpack(top_all[q]) for q in range(SHARE)], axis=0)
    parent = wide(nt, parent, tra[0])
    parent = wide(nt, parent, tra[1 + col // 2])
    parent = wide(nt, parent, tra[3 + col])
    parent = wide(nt, parent, tra[pl.ds(7 + 2 * col, 2)].reshape(128, 64))
    from_top = []
    for a in range(2):
        w = tra[pl.ds(15 + 4 * col + 2 * a, 2)].reshape(128, 64)
        from_top.append(wide(nt, parent[:, 64 * a : 64 * (a + 1)], w))

    for copy in copies:
        copy.wait()


    def arrived(kind):
        def wait(r, carry):
            x_at, core_at, cpl_at = in_plane(r)
            from_core = x_at * 2 + core_at
            many = DEPTH - 1 if kind == 0 else 1
            slots = pl.ds(kind * (DEPTH - 1), many)
            first = from_core * DEPTH + kind * (DEPTH - 1)
            pltpu.make_async_remote_copy(
                src_ref=outgoing.at[r, slots],
                dst_ref=incoming.at[
                    pl.ds(first, many),
                    pl.ds(pl.multiple_of(cpl_at * 16, 16), 16),
                ],
                send_sem=a2a_send.at[kind, r],
                recv_sem=a2a_recv.at[kind, from_core * SHARE + cpl_at],
                device_id=(leaf_at(x_at, z_by(far * kind), core_at), cpl_at),
                device_id_type=MESH,
            ).wait()
            return carry

        lax.fori_loop(1 if kind == 0 else 0, plane, wait, 0)

    for kind in range(2):
        arrived(kind)

    prefix[0] = jnp.zeros((64, 64), f32)

    def from_pair(j):
        return jnp.clip(index_s[0, j], 0, n_leaf - 1)

    def couple(u, acc):
        source = jnp.concatenate(
            [incoming[from_pair(2 * u)], incoming[from_pair(2 * u + 1)]], axis=1
        )
        matrix = jnp.concatenate([blocks[2 * u], blocks[2 * u + 1]], axis=1)
        acc = acc + nt(source, matrix)
        prefix[u + 1] = acc
        return acc

    lax.fori_loop(0, STEPS, couple, jnp.zeros((64, 64), f32), unroll=True)

    def run(m):
        return jnp.clip(start_s[m, 0], 0, STEPS)

    def field(m):
        return prefix[run(m + 1)] - prefix[run(m)]

    def pair(a, b):
        return jnp.concatenate([field(a), field(b)], axis=1)

    line = pair(1, 2) + wide(nt, field(0), tra[1:3].reshape(128, 64))
    lines = [line]
    for level in range(2, 5):
        first = (1 << level) - 1
        lower = []
        for j, tile in enumerate(lines):
            both = wide(nt, tile, lifts[len(lines) - 1 + j])
            lower.append(pair(first + 4 * j, first + 4 * j + 1) + both[:, :128])
            lower.append(pair(first + 4 * j + 2, first + 4 * j + 3) + both[:, 128:])
        lines = lower
    for j, tile in enumerate(lines):
        leaf_f[j] = tile
        leaf_b[j] = tile.astype(bf16)

    def field_copy(step, source):
        return pltpu.make_async_remote_copy(
            src_ref=leaf_b.at[pl.ds(2 * other(step), 2)],
            dst_ref=leaf_in.at[source],
            send_sem=field_send.at[step],
            recv_sem=field_recv.at[source],
            device_id=(me, other(step)),
            device_id_type=MESH,
        )

    for step in range(1, SHARE):
        field_copy(step, col).start()
    for step in range(1, SHARE):
        field_copy(step, other(step)).wait()

    for a in range(2):
        leaf = leaf_f[2 * col + a] + from_top[a]
        for step in range(1, SHARE):
            leaf = leaf + leaf_in[other(step), a].astype(f32)
        b = bas[:, pl.ds(pl.multiple_of(col * 256 + 128 * a, 128), 128)]
        out_ref[:, 128 * a : 128 * (a + 1)] = near_ref[:, 128 * a : 128 * (a + 1)] + nn(
            leaf.astype(bf16), spread(b)
        )


def body(
    vectors, embeddings, basis, transfer, coupling, top_transfer, top_coupling,
    send_boxes, block_slot, block_target,
):
    n_leaf = lax.axis_size("leaf")
    tops = top_transfer.shape[0]
    plane = 2 * (n_leaf // GROUP) * SHARE
    hbm = pl.BlockSpec(memory_space=pl.ANY)
    vmem = pl.BlockSpec(memory_space=pltpu.VMEM)
    dma = pltpu.SemaphoreType.DMA
    result = pl.pallas_call(
        functools.partial(kernel, n_leaf),
        out_shape=jax.ShapeDtypeStruct((NRHS, SHARE * LEAF), f32),
        in_specs=[hbm] * 10,
        out_specs=vmem,
        scratch_shapes=[
            pltpu.VMEM((64, 1280), bf16),
            pltpu.VMEM((64, 1280), bf16),
            pltpu.VMEM((64, 1024), bf16),
            pltpu.VMEM((BOX, 64, 64), bf16),
            pltpu.VMEM((64, 64, BLK), bf16),
            pltpu.VMEM((tops, 64, 64), bf16),
            pltpu.VMEM((tops, 64, 64), bf16),
            pltpu.VMEM((16, 64, 128), bf16),
            pltpu.VMEM((7, 16, 16, 128), bf16),
            pltpu.VMEM((32, 16, 128), bf16),
            pltpu.VMEM((plane, GROUP // 2, 16, 128), bf16),
            pltpu.VMEM((n_leaf, 64, 128), bf16),
            pltpu.VMEM((64, 128), f32),
            pltpu.VMEM((1, BLK), i32),
            pltpu.VMEM((1, BLK), i32),
            pltpu.VMEM((1, 2 * n_leaf), i32),
            pltpu.VMEM((SHARE, GROUP // 2, 2 * n_leaf), i32),
            pltpu.VMEM((SHARE * GROUP // 2, 2 * n_leaf), i32),
            pltpu.SMEM((SHARE * GROUP // 2, 2 * n_leaf), i32),
            pltpu.VMEM((7, 256, 128), bf16),
            pltpu.VMEM((8, 128), f32),
            pltpu.VMEM((GROUP, 8, 128), f32),
            pltpu.VMEM((GROUP, 16, 64), f32),
            pltpu.VMEM((8, 128), f32),
            pltpu.VMEM((n_leaf // GROUP, 8, 128), f32),
            pltpu.VMEM((2 * n_leaf // GROUP, 16, 64), f32),
            pltpu.VMEM((8, 128), f32),
            pltpu.VMEM((SHARE, 8, 128), f32),
            pltpu.VMEM((8, POS), i32),
            pltpu.VMEM((32, 128), i32),
            pltpu.SMEM((8, POS), i32),
            pltpu.SMEM((32, 128), i32),
            pltpu.VMEM((POS * 65 + 65, 128), f32),
            pltpu.VMEM((POS, 64, 128), bf16),
            pltpu.VMEM((STEPS + 1, 64, 64), f32),
            pltpu.VMEM((B_DEV // 2, 64, 128), f32),
            pltpu.VMEM((B_DEV // 2, 64, 128), bf16),
            pltpu.VMEM((SHARE, 2, 64, 128), bf16),
            pltpu.VMEM((64, SHARE * LEAF), f32),
            dma((13,)),
            dma((4,)),
            dma((4,)),
            dma((7 * SHARE,)),
            dma((SHARE * DEPTH,)),
            dma((7,)),
            dma((7,)),
            dma((2, plane)),
            dma((2, plane)),
            dma((GROUP,)),
            dma((GROUP,)),
            dma((n_leaf // GROUP,)),
            dma((n_leaf // GROUP,)),
            dma((SHARE,)),
            dma((SHARE,)),
            dma((SHARE,)),
            dma((SHARE,)),
        ],
        compiler_params=pltpu.CompilerParams(
            collective_id=0, has_side_effects=True, vmem_limit_bytes=56 * 1024 * 1024
        ),
    )(
        vectors.T, embeddings.T, basis.T, transfer, jnp.transpose(coupling, (1, 2, 0)),
        top_transfer, top_coupling, send_boxes,
        block_slot.reshape(1, BLK), block_target.reshape(1, BLK),
    )
    return result.T


def solution(mesh):
    placed = (
        P("leaf", None),
        P("leaf", None),
        P("leaf", None),
        P("leaf", None, None),
        P(("leaf", "cpl"), None, None),
        P(),
        P(),
        P("leaf", "cpl", None),
        P(("leaf", "cpl")),
        P(("leaf", "cpl")),
    )
    return jax.shard_map(
        body, mesh=mesh, in_specs=placed, out_specs=P(("leaf", "cpl"), None), check_vma=False
    )
```
